256 devices in a mesh: dp: 8 (over z), graph: 32 (over x, y, core).
Axes of the slice: x: 4, y: 4, z: 8, core: 2. Of those that a mesh axis runs over, the one named last changes fastest.
Arguments:
- node_feats: bfloat16 [8, 224, 49, 256], P('dp', 'graph'), may hold values from -0.125 to 0.125
- node_grads: bfloat16 [8, 224, 49, 256], P('dp', 'graph'), may hold values from -1.75 to 1.75
- node_row: int32 [8, 224], P('dp'), may hold values from 0 to 223, as said below
- edge_src: int32 [8, 16384], P('dp', 'graph'), may hold values from 0 to 223, as said below
- edge_tgt: int32 [8, 16384], P('dp', 'graph'), may hold values from 0 to 223, as said below
- edge_rot: int32 [8, 16384], P('dp', 'graph'), may hold values from 0 to 2047
- edge_len: float32 [8, 16384], P('dp', 'graph'), may hold values from 0.5 to 11.5
- edge_count: int32 [8, 32], P('dp', 'graph'), may hold values from 64 to 512, as said below
- rotations: bfloat16 [2048, 7, 49], replicated, as said below
- w_zero: bfloat16 [1792, 1792], replicated, may hold values from -0.125 to 0.125
- w_radial: float32 [600, 256], replicated, may hold values from -3 to 3
Outputs:
- node_grad: float32 [8, 224, 49, 256], P('dp', 'graph')
- weight_grad: float32 [1792, 1792], P('graph')
The draws below stay inside these ranges and needn't reach their ends.
Inputs may be any that keep to these rules, and one draw needn't show every extreme that they name: Each row of node_row is a permutation: atom i of a batch graph is held at row node_row[b, i], and graph index g holds rows g * 7 to (g + 1) * 7 - 1. `edge_tgt`: for every slot of the block of graph index g, the target atom is held at one of the rows g * 7 to (g + 1) * 7 - 1. `edge_src`: among the 512 slots of the block of one index of graph, at most 24 have source atoms held by the same index of graph; in every batch graph one index of graph holds the source atoms of exactly 24 live slots of every block. The first edge_count[b, g] slots of a block are live, the others are padding with valid ids; in every batch graph one index of graph has all 512 slots live. `rotations`: row l of each rotation is zero outside the coefficients of degree l (coefficients l * l to l * l + 2 l).
All inputs are finite; a program needn't handle non-finite values.
Results may differ from the reference program's by a relative error of at most 0.0041.
Values may be sent and summed in bfloat16 or wider, within the bound.
A program may use at most 256 MiB of HBM per device.

```python
import jax
import jax.numpy as jnp
from jax import lax

CHANNELS = 256
DEGREES = 7
GAUSSIANS = 600
COEFFS = 49
ROTATIONS = 2048
NODE_DEV = 7
EDGE_DEV = 512
BATCHES = 8
NODES = 224
EDGES = 16384
CAP = 24
MINLIVE = 64


def layout(key):
    subkeys = jax.random.split(jax.random.fold_in(key, 11), BATCHES)

    def shuffle(subkey):
        return jax.random.permutation(subkey, NODES)
    placed = jax.vmap(shuffle)(subkeys).astype(jnp.int32)
    inverse = jnp.argsort(placed, axis=1).astype(jnp.int32)
    owner_rows = jnp.arange(EDGES, dtype=jnp.int32) // EDGE_DEV * NODE_DEV
    owner_rows = owner_rows[None, :] + jax.random.randint(jax.random.fold_in(key, 12), (BATCHES, EDGES), 0, NODE_DEV, dtype=jnp.int32)
    targets = jnp.take_along_axis(inverse, owner_rows, axis=1)
    return (placed, inverse, targets.astype(jnp.int32))


def draw_node_row(key, part):
    return layout(key)[0]


def draw_edge_tgt(key, part):
    return layout(key)[2]


def draw_edge_src(key, part):
    inverse = layout(key)[1]
    groups = EDGES // EDGE_DEV
    cells = groups * CAP
    first_holder = jax.random.randint(jax.random.fold_in(key, 31), (BATCHES,), 0, groups, dtype=jnp.int32)
    block_keys = jax.random.split(jax.random.fold_in(key, 32), BATCHES * groups)

    def one_block(block_key):
        key_cells, key_front, key_back = jax.random.split(block_key, 3)
        others = jax.random.permutation(key_cells, cells - CAP).astype(jnp.int32) + CAP
        chosen = jnp.concatenate([jnp.arange(CAP, dtype=jnp.int32), others[:EDGE_DEV - CAP]])
        front = jax.random.permutation(key_front, MINLIVE).astype(jnp.int32)
        back = MINLIVE + jax.random.permutation(key_back, EDGE_DEV - MINLIVE).astype(jnp.int32)
        order = jnp.concatenate([front, back])
        return chosen[order] // CAP
    relative = jax.vmap(one_block)(block_keys).reshape(BATCHES, EDGES)
    holders = (relative + first_holder[:, None]) % groups
    within = jax.random.randint(jax.random.fold_in(key, 33), (BATCHES, EDGES), 0, NODE_DEV, dtype=jnp.int32)
    return jnp.take_along_axis(inverse, holders * NODE_DEV + within, axis=1).astype(jnp.int32)


def draw_edge_count(key, part):
    groups = EDGES // EDGE_DEV
    drawn = jax.random.randint(jax.random.fold_in(key, 21), (BATCHES, groups), MINLIVE, EDGE_DEV * 3 // 4 + 1, dtype=jnp.int32)
    fullest = jax.random.randint(jax.random.fold_in(key, 22), (BATCHES, 1), 0, groups, dtype=jnp.int32)
    positions = jnp.arange(groups, dtype=jnp.int32)[None, :]
    return jnp.where(positions == fullest, EDGE_DEV, drawn).astype(jnp.int32)


def draw_rotations(key, part):
    positions = jnp.arange(COEFFS, dtype=jnp.int32)
    squares = (jnp.arange(1, DEGREES, dtype=jnp.int32) ** 2)[None, :]
    degree = jnp.sum((positions[:, None] >= squares).astype(jnp.int32), axis=1)
    in_block = (degree[None, :] == jnp.arange(DEGREES, dtype=jnp.int32)[:, None]).astype(jnp.float32)
    factor = 1.0 / jnp.sqrt(2.0 * degree.astype(jnp.float32) + 1.0)
    values = jax.random.normal(key, (ROTATIONS, DEGREES, COEFFS), jnp.float32)
    return (values * factor[None, None, :] * in_block[None, :, :]).astype(jnp.bfloat16)


def place_ends(result, key, smallest, largest):
    spot = [jax.random.randint(jax.random.fold_in(key, axis), (), 0, length) for axis, length in enumerate(result.shape)]
    longest = result.shape.index(max(result.shape))
    next_to = spot[:longest] + [(spot[longest] + 1) % result.shape[longest]] + spot[longest + 1:]
    return result.at[tuple(spot)].set(smallest).at[tuple(next_to)].set(largest)


def steps_of(key, extent, cuts, smallest, largest):
    def one(axis_at, shards_of):
        heights = jax.random.uniform(jax.random.fold_in(jax.random.fold_in(key, 6), axis_at), (shards_of,), jnp.float32, smallest / len(cuts), largest / len(cuts))
        return jnp.repeat(jnp.exp(heights), extent[axis_at] // shards_of).reshape((-1,) + (1,) * (len(extent) - axis_at - 1))

    loudness = one(*cuts[0])
    for cut in cuts[1:]:
        loudness = loudness * one(*cut)
    return loudness


def bell_draw(rng, shape, deviation, limit, shards=(), held_as=jnp.bfloat16):
    gain = steps_of(rng, shape, shards, -0.22, 0.18) if shards else 1.0
    drawn = jax.random.normal(rng, shape, jnp.float32) * deviation * gain
    return jnp.minimum(jnp.maximum(drawn, -limit), limit).astype(held_as)


def setup_inputs(seed: int = 0) -> dict:
    keys = jax.random.split(jax.random.key(seed), 12)
    node_feats = bell_draw(keys[0], (BATCHES, NODES, COEFFS, CHANNELS), 0.02, 0.125, ((0, 8), (1, 32)))
    node_grads = bell_draw(keys[1], (BATCHES, NODES, COEFFS, CHANNELS), 0.3, 1.75, ((0, 8), (1, 32)))
    node_row = draw_node_row(jax.random.fold_in(keys[11], 71), 0)
    edge_src = draw_edge_src(jax.random.fold_in(keys[11], 71), 0)
    edge_tgt = draw_edge_tgt(jax.random.fold_in(keys[11], 71), 0)
    edge_rot = place_ends(jax.random.randint(keys[5], (BATCHES, EDGES), 0, ROTATIONS), jax.random.fold_in(keys[5], 1), 0, ROTATIONS - 1).astype(jnp.int32)
    edge_len = jnp.clip(0.5 + 11.0 * jax.random.uniform(keys[6], (BATCHES, EDGES), jnp.float32) ** steps_of(keys[6], (BATCHES, EDGES), ((0, 8), (1, 32)), -0.2, 0.2), 0.5, 11.5)
    edge_count = draw_edge_count(jax.random.fold_in(keys[11], 71), 0)
    rotations = draw_rotations(jax.random.fold_in(keys[11], 71), 0)
    w_zero = bell_draw(keys[9], (DEGREES * CHANNELS, DEGREES * CHANNELS), (DEGREES * CHANNELS) ** -0.5, 0.125)
    w_radial = bell_draw(keys[10], (GAUSSIANS, CHANNELS), 4 ** -0.5, 3.0, (), jnp.float32)
    return dict(node_feats=node_feats, node_grads=node_grads, node_row=node_row, edge_src=edge_src, edge_tgt=edge_tgt, edge_rot=edge_rot, edge_len=edge_len, edge_count=edge_count, rotations=rotations, w_zero=w_zero, w_radial=w_radial)


CUTOFF = 12.0


def radial_profile(lengths, w_radial):
    gauss_count = w_radial.shape[0]
    spacing = CUTOFF / (gauss_count - 1)
    centers = jnp.arange(gauss_count).astype(jnp.float32) * spacing
    basis = jnp.exp((-0.5 / (2.0 * spacing) ** 2) * (lengths[:, None] - centers[None, :]) ** 2)
    return jnp.dot(basis, w_radial, precision=lax.Precision.HIGHEST, preferred_element_type=jnp.float32)


def edge_terms(source, target, turn, radial, w_zero):
    turned = turn.astype(jnp.float32)
    rotated = jnp.einsum('bij,bjc->bic', turned, source.astype(jnp.float32))
    edge_in = (rotated * radial[:, None, :]).astype(jnp.bfloat16)
    edge_grad = jnp.einsum('bij,bjc->bic', turned, target.astype(jnp.float32)).astype(jnp.bfloat16)
    edge_rows = edge_in.shape[0]
    flat_in = edge_in.reshape(edge_rows, -1)
    flat_grad = edge_grad.reshape(edge_rows, -1)
    weight_term = jnp.dot(flat_in.T, flat_grad, preferred_element_type=jnp.float32)
    hidden = jnp.dot(flat_grad, w_zero.T, preferred_element_type=jnp.float32)
    returned = (hidden.reshape(edge_in.shape) * radial[:, None, :]).astype(jnp.bfloat16)
    node_term = jnp.einsum('bij,bic->bjc', turned, returned.astype(jnp.float32))
    return weight_term, node_term


def reference(node_feats, node_grads, node_row, edge_src, edge_tgt, edge_rot, edge_len, edge_count, rotations, w_zero, w_radial):
    square = w_zero.shape[0]
    weight_total = jnp.zeros((square, square), jnp.float32)
    outputs = []
    slots = jnp.arange(EDGES)
    blocks = EDGES // EDGE_DEV
    for batch_index in range(BATCHES):
        row_table = node_row[batch_index]
        source_rows = row_table[edge_src[batch_index]]
        target_rows = row_table[edge_tgt[batch_index]]
        live = ((slots % EDGE_DEV) < edge_count[batch_index][slots // EDGE_DEV]).astype(jnp.float32)
        radial = radial_profile(edge_len[batch_index], w_radial) * live[:, None]
        feats = node_feats[batch_index]
        grads = node_grads[batch_index]

        def advance(carry, pieces):
            weight_acc, node_acc = carry
            here_source, here_target, here_turn, here_radial = pieces
            weight_term, node_term = edge_terms(feats[here_source], grads[here_target], rotations[here_turn], here_radial, w_zero)
            return (weight_acc + weight_term, node_acc.at[here_source].add(node_term)), None

        pieces = (source_rows.reshape(blocks, EDGE_DEV), target_rows.reshape(blocks, EDGE_DEV),
                  edge_rot[batch_index].reshape(blocks, EDGE_DEV), radial.reshape(blocks, EDGE_DEV, -1))
        start_state = (weight_total, jnp.zeros(feats.shape, jnp.float32))
        (weight_total, node_acc), _ = lax.scan(advance, start_state, pieces)
        outputs.append(node_acc)
    return jnp.stack(outputs), weight_total
```

```python
import functools

import jax
import jax.numpy as jnp
from jax import lax
from jax.experimental import pallas as pl
from jax.experimental.pallas import tpu as pltpu
from jax.sharding import PartitionSpec as P

CUTOFF = 12.0
CAP = 24
DEG = 7
COEF = 49
ROWS = 7
CH = 256
WIDTH = DEG * CH
META = 128
WIDE = WIDTH + META
SPAN = 64 * ROWS
F32, BF16, I32 = jnp.float32, jnp.bfloat16, jnp.int32
MESH = pl.DeviceIdType.MESH
VMEM_LIMIT = 60 * 1024 * 1024


def iota(shape, dim):
    return lax.broadcasted_iota(I32, shape, dim)


def onehot(mask):
    return jnp.where(mask, 1.0, 0.0).astype(BF16)


def dot(a, b, dims=((1,), (0,))):
    return lax.dot_general(a, b, (dims, ((), ())), preferred_element_type=F32)


def spread_matrix():
    j, lane = iota((META, SPAN), 0), iota((META, SPAN), 1)
    return onehot((lane & 63 == j) & (j < COEF))


def selector(meta, column):
    wide = dot(meta.astype(BF16), spread_matrix())
    atom = meta[:, column : column + 1].astype(I32)
    return jnp.where(iota(wide.shape, 1) >> 6 == atom, wide, 0.0).astype(BF16)


def in_degree(position, degree):
    return (position >= degree * degree) & (position < (degree + 1) * (degree + 1))


def pack_nodes(nodes_ref, packed_ref):
    packed_ref[...] = jnp.zeros(packed_ref.shape, F32)
    for q in range(ROWS):
        packed_ref[q * 64 : q * 64 + COEF, :] = nodes_ref[q].astype(F32)


def send_rows_kernel(
    holders, count_ref, table_ref, src_ref, tgt_ref, rot_ref, len_ref, turns_ref, grads_ref,
    out_ref, turn_ref, rows_ref, packed_ref,
):
    own = lax.axis_index("graph")
    slots = src_ref.shape[1]
    atoms = table_ref.shape[1]
    rows = holders * CAP
    live = iota((1, slots), 1) < count_ref[0, 0]
    table = jnp.broadcast_to(table_ref[...].astype(F32), (8, atoms)).astype(BF16)

    def rows_of(ids):
        return dot(table, onehot(iota((atoms, slots), 0) == ids))[0:1].astype(I32)

    src = rows_of(src_ref[...])
    tgt = rows_of(tgt_ref[...])
    holder = (src * 9363) >> 16
    held = onehot((iota((holders, slots), 0) == holder) & live)
    before = onehot(iota((slots, slots), 0) < iota((slots, slots), 1))
    rank = jnp.sum(held.astype(F32) * dot(held, before), axis=0, keepdims=True)
    place = jnp.where(live, holder * CAP + rank.astype(I32), -1)
    chosen = onehot(iota((rows, slots), 0) == place)

    total = turns_ref[0].astype(F32)
    for degree in range(1, DEG):
        total += turns_ref[degree].astype(F32)
    turn_ref[...] = total.astype(BF16)
    step = 512
    turned = jnp.zeros((COEF, slots), F32)
    for first in range(0, turns_ref.shape[2], step):
        turned += dot(
            turn_ref[:, first : first + step],
            onehot(iota((step, slots), 0) + first == rot_ref[...]),
        )
    length = len_ref[...]
    high = length.astype(BF16).astype(F32)
    middle = (length - high).astype(BF16).astype(F32)
    rows_ref[...] = jnp.zeros(rows_ref.shape, F32)
    rows_ref[0:COEF, :] = turned
    rows_ref[49:50, :] = (src - holder * ROWS).astype(F32)
    rows_ref[50:51, :] = (tgt - own * ROWS).astype(F32)
    rows_ref[51:52, :] = jnp.ones((1, slots), F32)
    rows_ref[52:53, :] = high
    rows_ref[53:54, :] = middle
    rows_ref[54:55, :] = length - high - middle
    meta = dot(chosen, rows_ref[...].astype(BF16), ((1,), (1,)))

    pack_nodes(grads_ref, packed_ref)
    pick = selector(meta, 50)
    position = iota((SPAN, CH), 0) & 63
    for degree in range(DEG):
        part = jnp.where(in_degree(position, degree), packed_ref[...], 0.0).astype(BF16)
        grad = dot(pick, part)
        out_ref[:, :, degree * CH : (degree + 1) * CH] = grad.reshape(holders, CAP, CH).astype(BF16)
    out_ref[:, :, WIDTH:] = meta.reshape(holders, CAP, META).astype(BF16)


def exchange_kernel(n, x_ref, y_ref, keep_sem, send_sem, recv_sem):
    me = lax.axis_index("graph")
    barrier = pltpu.get_barrier_semaphore()

    def greet(k, _):
        pl.semaphore_signal(barrier, inc=1, device_id={"graph": lax.rem(me + k, n)}, device_id_type=MESH)
        return 0

    lax.fori_loop(1, n, greet, 0)
    keep = pltpu.make_async_copy(x_ref.at[me], y_ref.at[me], keep_sem)
    keep.start()
    pl.semaphore_wait(barrier, n - 1)

    def copy(k):
        peer = lax.rem(me + k, n)
        return pltpu.make_async_remote_copy(
            src_ref=x_ref.at[peer],
            dst_ref=y_ref.at[me],
            send_sem=send_sem.at[k],
            recv_sem=recv_sem.at[k],
            device_id={"graph": peer},
            device_id_type=MESH,
        )

    def begin(k, _):
        copy(k).start()
        return 0

    def landed(k, _):
        source = lax.rem(me - k + n, n)
        pltpu.make_async_remote_copy(
            src_ref=x_ref.at[source],
            dst_ref=y_ref.at[source],
            send_sem=send_sem.at[k],
            recv_sem=recv_sem.at[k],
            device_id={"graph": source},
            device_id_type=MESH,
        ).wait_recv()
        copy(k).wait_send()
        return 0

    lax.fori_loop(1, n, begin, 0)
    keep.wait()
    lax.fori_loop(1, n, landed, 0)


def edge_kernel(
    x_ref, feats_ref, w_ref, radial_ref, own_ref, other_ref, node_ref,
    packed_ref, grad_ref, in_ref, pick_ref, scale_ref, acc_ref,
):
    core = lax.rem(lax.axis_index("graph"), 2)
    rows = grad_ref.shape[0]
    half = WIDTH // 2
    for degree in range(DEG):
        cols = slice(degree * CH, (degree + 1) * CH)
        grad_ref[:, cols] = x_ref[:, :, cols].astype(F32).reshape(rows, CH).astype(BF16)
    meta = x_ref[:, :, WIDTH:].astype(F32).reshape(rows, META)
    lane = iota((rows, META), 1)
    length = jnp.sum(jnp.where((lane >= 52) & (lane < 55), meta, 0.0), axis=1, keepdims=True)
    live = meta[:, 51:52]
    gauss = radial_ref.shape[0]
    spacing = CUTOFF / (gauss - 1)
    centers = iota((1, gauss), 1).astype(F32) * spacing
    basis = jnp.exp((-0.5 / (2.0 * spacing) ** 2) * (length - centers) ** 2)
    scale_ref[...] = live * lax.dot_general(
        basis, radial_ref[...], (((1,), (0,)), ((), ())),
        precision=lax.Precision.HIGHEST, preferred_element_type=F32,
    )
    pick = selector(meta, 49)
    pick_ref[...] = pick.astype(F32).T.astype(BF16)
    pack_nodes(feats_ref, packed_ref)
    acc_ref[...] = jnp.zeros(acc_ref.shape, F32)
    position = iota((SPAN, CH), 0) & 63

    for degree in range(DEG):
        part = jnp.where(in_degree(position, degree), packed_ref[...], 0.0).astype(BF16)
        in_ref[:, degree * CH : (degree + 1) * CH] = (dot(pick, part) * scale_ref[...]).astype(BF16)

    def weights(degree, _):
        at = pl.ds(pl.multiple_of(degree * CH, CH), CH)
        turned = in_ref[:, at]
        mine = grad_ref[:, pl.ds(pl.multiple_of(core * half, 128), half)]
        own_ref[at, :] = dot(turned, mine, ((0,), (0,)))
        theirs = grad_ref[:, pl.ds(pl.multiple_of((1 - core) * half, 128), half)]
        other_ref[at, :] = dot(turned, theirs, ((0,), (0,))).astype(BF16)
        return 0

    lax.fori_loop(0, DEG, weights, 0)

    def backward(degree, _):
        at = pl.ds(pl.multiple_of(degree * CH, CH), CH)
        hidden = dot(grad_ref[...], w_ref[at, :], ((1,), (1,)))
        back = (hidden * scale_ref[...]).astype(BF16)
        term = dot(pick_ref[...], back)
        acc_ref[...] += jnp.where(in_degree(position, degree), term, 0.0)
        return 0

    lax.fori_loop(0, DEG, backward, 0)
    for q in range(ROWS):
        node_ref[q] = acc_ref[q * 64 : q * 64 + COEF, :]


def reduce_kernel(
    depth, own_ref, other_ref, out_ref,
    pair_ref, send1, recv1, acc, send2, recv2, total, send3, recv3, mine, recv4, whole, swap, both,
    ps, pr, s1, r1, s2, r2, s3, r3, s4, r4, s5, r5,
):
    me, layer = lax.axis_index("graph"), lax.axis_index("dp")
    core, place = lax.rem(me, 2), me // 2
    x, y = place // 4, lax.rem(place, 4)
    first = (1 - core) * x + core * y
    second = (1 - core) * y + core * x

    def chip(kind, a, b):
        return (1 - kind) * (a * 4 + b) + kind * (b * 4 + a)

    def along(k, m):
        a, b = lax.rem(first + k, 4), lax.rem(second + m, 4)
        return {"graph": chip(core, a, b) * 2 + core}

    partner = {"graph": place * 2 + 1 - core}

    def above(k):
        return {"dp": lax.rem(layer + k, depth)}

    barrier = pltpu.get_barrier_semaphore()
    peers = [partner] + [along(k, 0) for k in (1, 2, 3)] + [along(0, k) for k in (1, 2, 3)]
    peers += [above(k) for k in range(1, depth)]
    for peer in peers:
        pl.semaphore_signal(barrier, inc=1, device_id=peer, device_id_type=MESH)
    pl.semaphore_wait(barrier, len(peers))

    def remote(src, dst, ss, rs, peer):
        return pltpu.make_async_remote_copy(
            src_ref=src, dst_ref=dst, send_sem=ss, recv_sem=rs, device_id=peer, device_id_type=MESH
        )

    def pair(n):
        k, i = lax.rem(n // 4 + 1, 4), lax.rem(n, 4)
        block = chip(1 - core, lax.rem(second + k, 4), i)
        return remote(other_ref.at[block], pair_ref.at[n], ps.at[n], pr.at[n], partner)

    def pair_start(n, _):
        pair(n).start()
        return 0

    lax.fori_loop(0, 16, pair_start, 0)

    def out1(k, i):
        return remote(send1.at[k - 1, i], recv1.at[k - 1, i], s1.at[k - 1, i], r1.at[k - 1, i], along(k, 0))

    for k in (1, 2, 3):

        def step1(i, _, k=k):
            n = (k - 1) * 4 + i
            pair(n).wait_recv()
            block = chip(core, lax.rem(first + k, 4), i)
            send1[k - 1, i] = (own_ref[block] + pair_ref[n].astype(F32)).astype(BF16)
            out1(k, i).start()
            return 0

        lax.fori_loop(0, 4, step1, 0)

    def keep1(i, _):
        pair(12 + i).wait_recv()
        acc[i] = own_ref[chip(core, first, i)] + pair_ref[12 + i].astype(F32)
        return 0

    lax.fori_loop(0, 4, keep1, 0)

    def gathered(i):
        for k in (1, 2, 3):
            out1(k, i).wait_recv()
        got = acc[i]
        for k in (0, 1, 2):
            got += recv1[k, i].astype(F32)
        return got

    def out2(m):
        return remote(send2.at[m - 1], recv2.at[m - 1], s2.at[m - 1], r2.at[m - 1], along(0, m))

    for m in (1, 2, 3):
        send2[m - 1] = gathered(lax.rem(second + m, 4)).astype(BF16)
        out2(m).start()
    kept = gathered(second)
    for m in (1, 2, 3):
        out2(m).wait_recv()
        kept += recv2[m - 1].astype(F32)
    rows = kept.shape[0]
    total[0:rows, :] = kept
    total[rows:, :] = jnp.zeros((total.shape[0] - rows, kept.shape[1]), F32)
    send3[...] = total[...].astype(BF16).reshape(send3.shape)

    def out3(k):
        return remote(
            send3.at[lax.rem(layer + k, depth)], recv3.at[k - 1], s3.at[k - 1], r3.at[k - 1], above(k)
        )

    for k in range(1, depth):
        out3(k).start()
    part = total[pl.ds(pl.multiple_of(layer * 16, 16), 16), :]
    for k in range(1, depth):
        out3(k).wait_recv()
        part += recv3[k - 1].astype(F32)
    mine[...] = part.astype(BF16)

    def out4(k):
        return remote(mine, recv4.at[k - 1], s4.at[k - 1], r4.at[k - 1], above(k))

    for k in range(1, depth):
        out4(k).start()
    whole[layer] = mine[...]
    for k in range(1, depth):
        out4(k).wait_recv()
        whole[lax.rem(layer - k + depth, depth)] = recv4[k - 1]
    out5 = remote(whole, swap, s5, r5, partner)
    out5.start()
    half = kept.shape[1]
    row = pl.ds(pl.multiple_of(core * 56, 8), 56)
    both[...] = whole[...].astype(F32).reshape(both.shape)
    out_ref[:, pl.ds(pl.multiple_of(core * half, 128), half)] = both[row, :]
    out5.wait_recv()
    both[...] = swap[...].astype(F32).reshape(both.shape)
    out_ref[:, pl.ds(pl.multiple_of((1 - core) * half, 128), half)] = both[row, :]

    def pair_done(n, _):
        pair(n).wait_send()
        return 0

    lax.fori_loop(0, 16, pair_done, 0)
    for k in (1, 2, 3):
        for i in range(4):
            out1(k, i).wait_send()
        out2(k).wait_send()
    for k in range(1, depth):
        out3(k).wait_send()
        out4(k).wait_send()
    out5.wait_send()


def vmem():
    return pl.BlockSpec(memory_space=pltpu.VMEM)


def per_device(
    node_feats, node_grads, node_row, edge_src, edge_tgt, edge_rot, edge_len, edge_count, rotations, w_zero, w_radial,
    holders, depth,
):
    slots = edge_src.shape[1]
    turns = rotations.transpose(1, 2, 0)
    rows = holders * CAP
    half = WIDTH // 2
    params = functools.partial(pltpu.CompilerParams, vmem_limit_bytes=VMEM_LIMIT)
    wide = jax.ShapeDtypeStruct((holders, CAP, WIDE), BF16)
    sent = pl.pallas_call(
        functools.partial(send_rows_kernel, holders),
        out_shape=wide,
        in_specs=[pl.BlockSpec(memory_space=pltpu.SMEM)] + [vmem()] * 7,
        out_specs=vmem(),
        scratch_shapes=[
            pltpu.VMEM((COEF, turns.shape[2]), BF16),
            pltpu.VMEM((META, slots), F32),
            pltpu.VMEM((SPAN, CH), F32),
        ],
        compiler_params=params(),
        name="send_rows",
    )(edge_count, node_row, edge_src, edge_tgt, edge_rot, edge_len, turns, node_grads[0])
    anywhere = pl.BlockSpec(memory_space=pl.ANY)
    dma = pltpu.SemaphoreType.DMA
    got = pl.pallas_call(
        functools.partial(exchange_kernel, holders),
        out_shape=wide,
        in_specs=[anywhere],
        out_specs=anywhere,
        scratch_shapes=[dma, dma((holders,)), dma((holders,))],
        compiler_params=pltpu.CompilerParams(collective_id=0, has_side_effects=True),
        name="exchange",
    )(sent)
    own, other, node = pl.pallas_call(
        edge_kernel,
        out_shape=(
            jax.ShapeDtypeStruct((WIDTH, half), F32),
            jax.ShapeDtypeStruct((WIDTH, half), BF16),
            jax.ShapeDtypeStruct((ROWS, COEF, CH), F32),
        ),
        in_specs=[vmem()] * 4,
        out_specs=(vmem(),) * 3,
        scratch_shapes=[
            pltpu.VMEM((SPAN, CH), F32),
            pltpu.VMEM((rows, WIDTH), BF16),
            pltpu.VMEM((rows, WIDTH), BF16),
            pltpu.VMEM((SPAN, rows), BF16),
            pltpu.VMEM((rows, CH), F32),
            pltpu.VMEM((SPAN, CH), F32),
        ],
        compiler_params=params(),
        name="edges",
    )(got, node_feats[0], w_zero, w_radial)
    chips = holders // 2
    tall = WIDTH // chips
    block = (tall, half)
    weight = pl.pallas_call(
        functools.partial(reduce_kernel, depth),
        out_shape=jax.ShapeDtypeStruct((WIDTH // holders, WIDTH), F32),
        in_specs=[vmem(), anywhere],
        out_specs=vmem(),
        scratch_shapes=[
            pltpu.VMEM((chips, *block), BF16),
            pltpu.VMEM((3, 4, *block), BF16),
            pltpu.VMEM((3, 4, *block), BF16),
            pltpu.VMEM((4, *block), F32),
            pltpu.VMEM((3, *block), BF16),
            pltpu.VMEM((3, *block), BF16),
            pltpu.VMEM((depth * 16, half), F32),
            pltpu.VMEM((depth, 16, half), BF16),
            pltpu.VMEM((depth - 1, 16, half), BF16),
            pltpu.VMEM((16, half), BF16),
            pltpu.VMEM((depth - 1, 16, half), BF16),
            pltpu.VMEM((depth, 16, half), BF16),
            pltpu.VMEM((depth, 16, half), BF16),
            pltpu.VMEM((depth * 16, half), F32),
            dma((16,)), dma((16,)),
            dma((3, 4)), dma((3, 4)),
            dma((3,)), dma((3,)),
            dma((depth - 1,)), dma((depth - 1,)),
            dma((depth - 1,)), dma((depth - 1,)),
            dma, dma,
        ],
        compiler_params=params(collective_id=1, has_side_effects=True),
        name="reduce_weights",
    )(own.reshape(chips, *block), other.reshape(chips, *block))
    return (node[None], weight)


def solution(mesh):
    graph = P("dp", "graph")
    placed = (
        P("dp", "graph", None, None), P("dp", "graph", None, None), P("dp", None),
        graph, graph, graph, graph, graph, P(), P(), P(),
    )
    return jax.shard_map(
        functools.partial(per_device, holders=mesh.shape["graph"], depth=mesh.shape["dp"]),
        mesh=mesh,
        in_specs=placed,
        out_specs=(P("dp", "graph", None, None), P("graph", None)),
        check_vma=False,
    )
```

```python
import functools

import jax
import jax.numpy as jnp
from jax import lax
from jax.experimental import pallas as pl
from jax.experimental.pallas import tpu as pltpu
from jax.sharding import PartitionSpec as P

CUTOFF = 12.0
CAP = 24
DEG = 7
COEF = 49
ROWS = 7
CH = 256
WIDTH = DEG * CH
META = 128
HALF = WIDTH // 2
TALL = 112
SPAN = 64 * ROWS
F32, BF16, I32 = jnp.float32, jnp.bfloat16, jnp.int32
MESH = pl.DeviceIdType.MESH
VMEM_LIMIT = 60 * 1024 * 1024
FAR = (
    (2, 2), (2, 1), (1, 2), (2, 3), (3, 2), (2, 0), (0, 2), (1, 1),
    (3, 3), (1, 3), (3, 1), (1, 0), (0, 1), (3, 0), (0, 3),
)
STEPS = [(a, b, c) for c in (0, 1) for a, b in FAR] + [(0, 0, 1)]


def iota(shape, dim):
    return lax.broadcasted_iota(I32, shape, dim)


def onehot(mask):
    return jnp.where(mask, 1.0, 0.0).astype(BF16)


def dot(a, b, dims=((1,), (0,))):
    return lax.dot_general(a, b, (dims, ((), ())), preferred_element_type=F32)


def spread_matrix():
    j, lane = iota((META, SPAN), 0), iota((META, SPAN), 1)
    return onehot((lane & 63 == j) & (j < COEF))


def selector(meta, column):
    wide = dot(meta.astype(BF16), spread_matrix())
    atom = meta[:, column : column + 1].astype(I32)
    return jnp.where(iota(wide.shape, 1) >> 6 == atom, wide, 0.0).astype(BF16)


def in_degree(position, degree):
    return (position >= degree * degree) & (position < (degree + 1) * (degree + 1))


def pack_nodes(nodes_ref, packed_ref):
    packed_ref[...] = jnp.zeros(packed_ref.shape, F32)
    for q in range(ROWS):
        packed_ref[q * 64 : q * 64 + COEF, :] = nodes_ref[q].astype(F32)


def find_meta(holders, count_ref, table_ref, src_ref, tgt_ref, rot_ref, len_ref, turns_ref, turn_ref, rows_ref):
    own = lax.axis_index("graph")
    slots = src_ref.shape[1]
    atoms = table_ref.shape[1]
    live = iota((1, slots), 1) < count_ref[0, 0]
    table = jnp.broadcast_to(table_ref[...].astype(F32), (8, atoms)).astype(BF16)

    def rows_of(ids):
        return dot(table, onehot(iota((atoms, slots), 0) == ids))[0:1].astype(I32)

    src = rows_of(src_ref[...])
    tgt = rows_of(tgt_ref[...])
    holder = (src * 9363) >> 16
    held = onehot((iota((holders, slots), 0) == holder) & live)
    before = onehot(iota((slots, slots), 0) < iota((slots, slots), 1))
    rank = jnp.sum(held.astype(F32) * dot(held, before), axis=0, keepdims=True)
    place = jnp.where(live, holder * CAP + rank.astype(I32), -1)
    chosen = onehot(iota((holders * CAP, slots), 0) == place)

    total = turns_ref[0].astype(F32)
    for degree in range(1, DEG):
        total += turns_ref[degree].astype(F32)
    turn_ref[...] = total.astype(BF16)
    step = 512
    turned = jnp.zeros((COEF, slots), F32)
    for start in range(0, turns_ref.shape[2], step):
        turned += dot(
            turn_ref[:, start : start + step],
            onehot(iota((step, slots), 0) + start == rot_ref[...]),
        )
    length = len_ref[...]
    high = length.astype(BF16).astype(F32)
    middle = (length - high).astype(BF16).astype(F32)
    rows_ref[...] = jnp.zeros(rows_ref.shape, F32)
    rows_ref[0:COEF, :] = turned
    rows_ref[49:50, :] = (src - holder * ROWS).astype(F32)
    rows_ref[50:51, :] = (tgt - own * ROWS).astype(F32)
    rows_ref[51:52, :] = jnp.ones((1, slots), F32)
    rows_ref[52:53, :] = high
    rows_ref[53:54, :] = middle
    rows_ref[54:55, :] = length - high - middle
    return dot(chosen, rows_ref[...].astype(BF16), ((1,), (1,)))


def layer_kernel(
    holders, depth,
    count_ref, table_ref, src_ref, tgt_ref, rot_ref, len_ref, turns_ref, grads_ref, feats_ref, radial_ref, w_hbm,
    node_ref, out_ref,
    turn_ref, rows_ref, packed_ref, meta_out, meta_in, grad_out, grad_in, w_ref,
    grad_ref, in_ref, pick_ref, scale_ref, acc_ref, own_ref, other_ref,
    pair_ref, send1, recv1, part1, send2, recv2, total, send3, recv3, mine, recv4, whole, swap, both,
    ws, ms, mr, gs, gr, ps, pr, s1, r1, s2, r2, s3, r3, s4, r4, s5, r5,
):
    me, layer = lax.axis_index("graph"), lax.axis_index("dp")
    core, place = lax.rem(me, 2), me // 2
    x, y = place // 4, lax.rem(place, 4)
    rows = holders * CAP
    first = (1 - core) * x + core * y
    second = (1 - core) * y + core * x

    def chip(kind, a, b):
        return (1 - kind) * (a * 4 + b) + kind * (b * 4 + a)

    def index(a, b, c):
        return chip(core, lax.rem(first + a, 4), lax.rem(second + b, 4)) * 2 + lax.rem(core + c, 2)

    def along(a, b):
        return {"graph": index(a, b, 0)}

    partner = {"graph": index(0, 0, 1)}

    def above(k):
        return {"dp": lax.rem(layer + k, depth)}

    def remote(src, dst, ss, rs, peer):
        return pltpu.make_async_remote_copy(
            src_ref=src, dst_ref=dst, send_sem=ss, recv_sem=rs, device_id=peer, device_id_type=MESH
        )

    load_w = pltpu.make_async_copy(w_hbm, w_ref, ws)
    load_w.start()
    barrier = pltpu.get_barrier_semaphore()
    for a, b, c in STEPS:
        pl.semaphore_signal(barrier, inc=1, device_id={"graph": index(a, b, c)}, device_id_type=MESH)
    for k in range(1, depth):
        pl.semaphore_signal(barrier, inc=1, device_id=above(k), device_id_type=MESH)

    meta = find_meta(
        holders, count_ref, table_ref, src_ref, tgt_ref, rot_ref, len_ref, turns_ref, turn_ref, rows_ref
    )
    meta_out[...] = meta.reshape(holders, CAP, META).astype(BF16)
    pl.semaphore_wait(barrier, len(STEPS) + depth - 1)

    def meta_copy(k):
        peer = index(*STEPS[k - 1])
        return remote(meta_out.at[peer], meta_in.at[k], ms.at[k], mr.at[k], {"graph": peer})

    def grad_copy(k):
        peer = index(*STEPS[k - 1])
        return remote(grad_out.at[peer], grad_in.at[k], gs.at[k], gr.at[k], {"graph": peer})

    for k in range(1, holders):
        meta_copy(k).start()
    pack_nodes(grads_ref, packed_ref)
    pick = selector(meta, 50)
    position = iota((SPAN, CH), 0) & 63
    for degree in range(DEG):
        part = jnp.where(in_degree(position, degree), packed_ref[...], 0.0).astype(BF16)
        grad = dot(pick, part)
        grad_out[:, :, degree * CH : (degree + 1) * CH] = grad.reshape(holders, CAP, CH).astype(BF16)
    for k in range(1, holders):
        grad_copy(k).start()
    meta_in[0] = meta_out[me]
    grad_in[0] = grad_out[me]

    for k in range(1, holders):
        meta_copy(k).wait_recv()
    meta = meta_in[...].astype(F32).reshape(rows, META)
    lane = iota((rows, META), 1)
    length = jnp.sum(jnp.where((lane >= 52) & (lane < 55), meta, 0.0), axis=1, keepdims=True)
    live = meta[:, 51:52]
    gauss = radial_ref.shape[0]
    spacing = CUTOFF / (gauss - 1)
    centers = iota((1, gauss), 1).astype(F32) * spacing
    basis = jnp.exp((-0.5 / (2.0 * spacing) ** 2) * (length - centers) ** 2)
    scale_ref[...] = live * lax.dot_general(
        basis, radial_ref[...], (((1,), (0,)), ((), ())),
        precision=lax.Precision.HIGHEST, preferred_element_type=F32,
    )
    pick = selector(meta, 49)
    pick_ref[...] = pick.astype(F32).T.astype(BF16)
    pack_nodes(feats_ref, packed_ref)
    for degree in range(DEG):
        part = jnp.where(in_degree(position, degree), packed_ref[...], 0.0).astype(BF16)
        in_ref[:, degree * CH : (degree + 1) * CH] = (dot(pick, part) * scale_ref[...]).astype(BF16)
    acc_ref[...] = jnp.zeros(acc_ref.shape, F32)
    for k in range(1, holders):
        grad_copy(k).wait_recv()
    for degree in range(DEG):
        cols = slice(degree * CH, (degree + 1) * CH)
        grad_ref[:, cols] = grad_in[:, :, cols].astype(F32).reshape(rows, CH).astype(BF16)

    def columns(kind):
        return pl.ds(pl.multiple_of(kind * HALF, 128), HALF)

    def weights_other(degree, _):
        at = pl.ds(pl.multiple_of(degree * CH, CH), CH)
        other_ref[at, :] = dot(in_ref[:, at], grad_ref[:, columns(1 - core)], ((0,), (0,))).astype(BF16)
        return 0

    lax.fori_loop(0, DEG, weights_other, 0)

    def block_of(kind, n):
        m, k = lax.rem(n // 4 + 1, 4), lax.rem(n + 1, 4)
        a = lax.rem((1 - kind) * x + kind * y + k, 4)
        b = lax.rem((1 - kind) * y + kind * x + m, 4)
        return pl.ds(pl.multiple_of(chip(kind, a, b) * TALL, 16), TALL)

    def pair(n):
        return remote(other_ref.at[block_of(1 - core, n)], pair_ref.at[n], ps.at[n], pr.at[n], partner)

    def pair_start(n, _):
        pair(n).start()
        return 0

    lax.fori_loop(0, 16, pair_start, 0)

    def weights_own(degree, _):
        at = pl.ds(pl.multiple_of(degree * CH, CH), CH)
        own_ref[at, :] = dot(in_ref[:, at], grad_ref[:, columns(core)], ((0,), (0,)))
        return 0

    lax.fori_loop(0, DEG, weights_own, 0)

    def paired(n):
        pair(n).wait_recv()
        return own_ref[block_of(core, n), :] + pair_ref[n].astype(F32)

    def out1(i, k):
        return remote(send1.at[i, k - 1], recv1.at[i, k - 1], s1.at[i, k - 1], r1.at[i, k - 1], along(k, 0))

    def step1(i, _):
        for k in (1, 2, 3):
            send1[i, k - 1] = paired(i * 4 + k - 1).astype(BF16)
            out1(i, k).start()
        part1[i] = paired(i * 4 + 3)
        return 0

    lax.fori_loop(0, 4, step1, 0)

    load_w.wait()

    def backward(degree, _):
        at = pl.ds(pl.multiple_of(degree * CH, CH), CH)
        hidden = dot(grad_ref[...], w_ref[at, :], ((1,), (1,)))
        back = (hidden * scale_ref[...]).astype(BF16)
        term = dot(pick_ref[...], back)
        acc_ref[...] += jnp.where(in_degree(position, degree), term, 0.0)
        return 0

    lax.fori_loop(0, DEG, backward, 0)
    for q in range(ROWS):
        node_ref[q] = acc_ref[q * 64 : q * 64 + COEF, :]

    def gathered(i):
        got = part1[i]
        for k in (1, 2, 3):
            out1(i, k).wait_recv()
            got += recv1[i, k - 1].astype(F32)
        return got

    def out2(m):
        return remote(send2.at[m - 1], recv2.at[m - 1], s2.at[m - 1], r2.at[m - 1], along(0, m))

    for m in (1, 2, 3):
        send2[m - 1] = gathered(m - 1).astype(BF16)
        out2(m).start()
    kept = gathered(3)
    for m in (1, 2, 3):
        out2(m).wait_recv()
        kept += recv2[m - 1].astype(F32)
    total[0:TALL, :] = kept
    total[TALL:, :] = jnp.zeros((total.shape[0] - TALL, HALF), F32)
    send3[...] = total[...].astype(BF16).reshape(send3.shape)

    def out3(k):
        return remote(
            send3.at[lax.rem(layer + k, depth)], recv3.at[k - 1], s3.at[k - 1], r3.at[k - 1], above(k)
        )

    for k in range(1, depth):
        out3(k).start()
    part = total[pl.ds(pl.multiple_of(layer * 16, 16), 16), :]
    for k in range(1, depth):
        out3(k).wait_recv()
        part += recv3[k - 1].astype(F32)
    mine[...] = part.astype(BF16)

    def out4(k):
        return remote(mine, recv4.at[k - 1], s4.at[k - 1], r4.at[k - 1], above(k))

    for k in range(1, depth):
        out4(k).start()
    whole[layer] = mine[...]
    for k in range(1, depth):
        out4(k).wait_recv()
        whole[lax.rem(layer - k + depth, depth)] = recv4[k - 1]
    out5 = remote(whole, swap, s5, r5, partner)
    out5.start()
    row = pl.ds(pl.multiple_of(core * 56, 8), 56)
    both[...] = whole[...].astype(F32).reshape(both.shape)
    out_ref[:, columns(core)] = both[row, :]
    out5.wait_recv()
    both[...] = swap[...].astype(F32).reshape(both.shape)
    out_ref[:, columns(1 - core)] = both[row, :]

    for k in range(1, holders):
        meta_copy(k).wait_send()
        grad_copy(k).wait_send()

    def pair_done(n, _):
        pair(n).wait_send()
        return 0

    lax.fori_loop(0, 16, pair_done, 0)
    for k in (1, 2, 3):
        for i in range(4):
            out1(i, k).wait_send()
        out2(k).wait_send()
    for k in range(1, depth):
        out3(k).wait_send()
        out4(k).wait_send()
    out5.wait_send()


def per_device(
    node_feats, node_grads, node_row, edge_src, edge_tgt, edge_rot, edge_len, edge_count, rotations, w_zero, w_radial,
    holders, depth,
):
    slots = edge_src.shape[1]
    turns = rotations.transpose(1, 2, 0)
    rows = holders * CAP
    block = (TALL, HALF)
    vmem = pl.BlockSpec(memory_space=pltpu.VMEM)
    dma = pltpu.SemaphoreType.DMA
    buffer = pltpu.VMEM
    node, weight = pl.pallas_call(
        functools.partial(layer_kernel, holders, depth),
        out_shape=(
            jax.ShapeDtypeStruct((ROWS, COEF, CH), F32),
            jax.ShapeDtypeStruct((WIDTH // holders, WIDTH), F32),
        ),
        in_specs=[pl.BlockSpec(memory_space=pltpu.SMEM)] + [vmem] * 9 + [pl.BlockSpec(memory_space=pl.ANY)],
        out_specs=(vmem, vmem),
        scratch_shapes=[
            buffer((COEF, turns.shape[2]), BF16),
            buffer((META, slots), F32),
            buffer((SPAN, CH), F32),
            buffer((holders, CAP, META), BF16),
            buffer((holders, CAP, META), BF16),
            buffer((holders, CAP, WIDTH), BF16),
            buffer((holders, CAP, WIDTH), BF16),
            buffer((WIDTH, WIDTH), BF16),
            buffer((rows, WIDTH), BF16),
            buffer((rows, WIDTH), BF16),
            buffer((SPAN, rows), BF16),
            buffer((rows, CH), F32),
            buffer((SPAN, CH), F32),
            buffer((WIDTH, HALF), F32),
            buffer((WIDTH, HALF), BF16),
            buffer((16, *block), BF16),
            buffer((4, 3, *block), BF16),
            buffer((4, 3, *block), BF16),
            buffer((4, *block), F32),
            buffer((3, *block), BF16),
            buffer((3, *block), BF16),
            buffer((depth * 16, HALF), F32),
            buffer((depth, 16, HALF), BF16),
            buffer((depth - 1, 16, HALF), BF16),
            buffer((16, HALF), BF16),
            buffer((depth - 1, 16, HALF), BF16),
            buffer((depth, 16, HALF), BF16),
            buffer((depth, 16, HALF), BF16),
            buffer((depth * 16, HALF), F32),
            dma,
            dma((holders,)), dma((holders,)),
            dma((holders,)), dma((holders,)),
            dma((16,)), dma((16,)),
            dma((4, 3)), dma((4, 3)),
            dma((3,)), dma((3,)),
            dma((depth - 1,)), dma((depth - 1,)),
            dma((depth - 1,)), dma((depth - 1,)),
            dma, dma,
        ],
        compiler_params=pltpu.CompilerParams(
            collective_id=0, has_side_effects=True, vmem_limit_bytes=VMEM_LIMIT
        ),
        name="layer",
    )(
        edge_count, node_row, edge_src, edge_tgt, edge_rot, edge_len, turns,
        node_grads[0], node_feats[0], w_radial, w_zero,
    )
    return (node[None], weight)


def solution(mesh):
    graph = P("dp", "graph")
    placed = (
        P("dp", "graph", None, None), P("dp", "graph", None, None), P("dp", None),
        graph, graph, graph, graph, graph, P(), P(), P(),
    )
    return jax.shard_map(
        functools.partial(per_device, holders=mesh.shape["graph"], depth=mesh.shape["dp"]),
        mesh=mesh,
        in_specs=placed,
        out_specs=(P("dp", "graph", None, None), P("graph", None)),
        check_vma=False,
    )
```

```python
import functools

import jax
import jax.numpy as jnp
from jax import lax
from jax.experimental import pallas as pl
from jax.experimental.pallas import tpu as pltpu
from jax.sharding import PartitionSpec as P

CUTOFF = 12.0
CAP = 24
DEG = 7
COEF = 49
ROWS = 7
CH = 256
WIDTH = DEG * CH
META = 128
HALF = WIDTH // 2
TALL = 112
PARTS = ((0, 512), (512, 384))
SPAN = 64 * ROWS
F32, BF16, I32 = jnp.float32, jnp.bfloat16, jnp.int32
MESH = pl.DeviceIdType.MESH
VMEM_LIMIT = 60 * 1024 * 1024
FAR = (
    (2, 2), (2, 1), (1, 2), (2, 3), (3, 2), (2, 0), (0, 2), (1, 1),
    (3, 3), (1, 3), (3, 1), (1, 0), (0, 1), (3, 0), (0, 3),
)
GROUPS = ((0, 16), (16, 26), (26, 32))
STEPS = [(a, b, c) for c in (0, 1) for a, b in FAR] + [(0, 0, 1)]


def iota(shape, dim):
    return lax.broadcasted_iota(I32, shape, dim)


def onehot(mask):
    return jnp.where(mask, 1.0, 0.0).astype(BF16)


def dot(a, b, dims=((1,), (0,))):
    return lax.dot_general(a, b, (dims, ((), ())), preferred_element_type=F32)


def spread_matrix():
    j, lane = iota((META, SPAN), 0), iota((META, SPAN), 1)
    return onehot((lane & 63 == j) & (j < COEF))


def selector(meta, column):
    wide = dot(meta.astype(BF16), spread_matrix())
    atom = meta[:, column : column + 1].astype(I32)
    return jnp.where(iota(wide.shape, 1) >> 6 == atom, wide, 0.0).astype(BF16)


def in_degree(position, degree):
    return (position >= degree * degree) & (position < (degree + 1) * (degree + 1))


def pack_nodes(nodes_ref, packed_ref):
    packed_ref[...] = jnp.zeros(packed_ref.shape, F32)
    for q in range(ROWS):
        packed_ref[q * 64 : q * 64 + COEF, :] = nodes_ref[q].astype(F32)


def find_meta(holders, count_ref, table_ref, src_ref, tgt_ref, rot_ref, len_ref, turns_ref, turn_ref, rows_ref):
    own = lax.axis_index("graph")
    slots = src_ref.shape[1]
    atoms = table_ref.shape[1]
    live = iota((1, slots), 1) < count_ref[0, 0]
    table = jnp.broadcast_to(table_ref[...].astype(F32), (8, atoms)).astype(BF16)

    def rows_of(ids):
        return dot(table, onehot(iota((atoms, slots), 0) == ids))[0:1].astype(I32)

    src = rows_of(src_ref[...])
    tgt = rows_of(tgt_ref[...])
    holder = (src * 9363) >> 16
    held = onehot((iota((holders, slots), 0) == holder) & live)
    before = onehot(iota((slots, slots), 0) < iota((slots, slots), 1))
    rank = jnp.sum(held.astype(F32) * dot(held, before), axis=0, keepdims=True)
    place = jnp.where(live, holder * CAP + rank.astype(I32), -1)
    chosen = onehot(iota((holders * CAP, slots), 0) == place)

    total = turns_ref[0].astype(F32)
    for degree in range(1, DEG):
        total += turns_ref[degree].astype(F32)
    turn_ref[...] = total.astype(BF16)
    step = 512
    turned = jnp.zeros((COEF, slots), F32)
    for start in range(0, turns_ref.shape[2], step):
        turned += dot(
            turn_ref[:, start : start + step],
            onehot(iota((step, slots), 0) + start == rot_ref[...]),
        )
    length = len_ref[...]
    high = length.astype(BF16).astype(F32)
    middle = (length - high).astype(BF16).astype(F32)
    rows_ref[...] = jnp.zeros(rows_ref.shape, F32)
    rows_ref[0:COEF, :] = turned
    rows_ref[49:50, :] = (src - holder * ROWS).astype(F32)
    rows_ref[50:51, :] = (tgt - own * ROWS).astype(F32)
    rows_ref[51:52, :] = jnp.ones((1, slots), F32)
    rows_ref[52:53, :] = high
    rows_ref[53:54, :] = middle
    rows_ref[54:55, :] = length - high - middle
    return dot(chosen, rows_ref[...].astype(BF16), ((1,), (1,)))


class PartSum:
    def __init__(self, at, width, own, remote, along, above, layer, depth, partner, first, second, core, refs):
        self.at, self.width, self.own, self.remote, self.along, self.above = at, width, own, remote, along, above
        self.layer, self.depth, self.partner, self.first, self.second, self.core = (
            layer, depth, partner, first, second, core
        )
        (
            self.send1, self.recv1, self.send2, self.recv2, self.total, self.send3, self.recv3,
            self.mine, self.recv4, self.whole, self.swap, self.both,
            self.s1, self.r1, self.s2, self.r2, self.s3, self.r3, self.s4, self.r4, self.s5, self.r5,
        ) = refs

    def block(self, k, m):
        a, b = lax.rem(self.first + k, 4), lax.rem(self.second + m, 4)
        place = (1 - self.core) * (a * 4 + b) + self.core * (b * 4 + a)
        return self.own[pl.ds(pl.multiple_of(place * TALL, 16), TALL), self.at : self.at + self.width]

    def out1(self, i, k):
        return self.remote(
            self.send1.at[k - 1, i], self.recv1.at[k - 1, i], self.s1.at[k - 1, i], self.r1.at[k - 1, i],
            self.along(k, 0),
        )

    def out2(self, m):
        return self.remote(
            self.send2.at[m - 1], self.recv2.at[m - 1], self.s2.at[m - 1], self.r2.at[m - 1], self.along(0, m)
        )

    def out3(self, k):
        to = lax.rem(self.layer + k, self.depth)
        return self.remote(
            self.send3.at[to], self.recv3.at[k - 1], self.s3.at[k - 1], self.r3.at[k - 1], self.above(k)
        )

    def out4(self, k):
        return self.remote(self.mine, self.recv4.at[k - 1], self.s4.at[k - 1], self.r4.at[k - 1], self.above(k))

    def out5(self):
        return self.remote(self.whole, self.swap, self.s5, self.r5, self.partner)

    def turns(self):
        return sorted(range(1, self.depth), key=lambda k: (-min(k, self.depth - k), k))

    def begin(self):
        def step(i, _):
            for k in (1, 3, 2):
                self.send1[k - 1, i] = self.block(k, i + 1).astype(BF16)
                self.out1(i, k).start()
            return 0

        lax.fori_loop(0, 4, step, 0)

    def gathered(self, i):
        got = self.block(0, i + 1)
        for k in (1, 2, 3):
            self.out1(i, k).wait_recv()
            got += self.recv1[k - 1, i].astype(F32)
        return got

    def second_axis(self):
        for m in (1, 3, 2):
            self.send2[m - 1] = self.gathered(m - 1).astype(BF16)
            self.out2(m).start()
        self.total[0:TALL, :] = self.gathered(3)
        self.total[TALL:, :] = jnp.zeros((self.total.shape[0] - TALL, self.width), F32)

    def over_layers(self):
        kept = self.total[0:TALL, :]
        for m in (1, 2, 3):
            self.out2(m).wait_recv()
            kept += self.recv2[m - 1].astype(F32)
        self.total[0:TALL, :] = kept
        self.send3[...] = self.total[...].astype(BF16).reshape(self.send3.shape)
        for k in self.turns():
            self.out3(k).start()

    def share(self):
        part = self.total[pl.ds(pl.multiple_of(self.layer * 16, 16), 16), :]
        for k in range(1, self.depth):
            self.out3(k).wait_recv()
            part += self.recv3[k - 1].astype(F32)
        self.mine[...] = part.astype(BF16)
        for k in self.turns():
            self.out4(k).start()
        self.whole[self.layer] = self.mine[...]

    def trade(self):
        for k in range(1, self.depth):
            self.out4(k).wait_recv()
            self.whole[lax.rem(self.layer - k + self.depth, self.depth)] = self.recv4[k - 1]
        self.out5().start()

    def finish(self, out_ref):
        row = pl.ds(pl.multiple_of(self.core * 56, 8), 56)
        for ref, kind in ((self.whole, self.core), (self.swap, 1 - self.core)):
            if ref is self.swap:
                self.out5().wait_recv()
            self.both[...] = ref[...].astype(F32).reshape(self.both.shape)
            out_ref[:, pl.ds(pl.multiple_of(kind * HALF + self.at, 128), self.width)] = self.both[row, :]

    def sent(self):
        for k in (1, 2, 3):
            for i in range(4):
                self.out1(i, k).wait_send()
            self.out2(k).wait_send()
        for k in range(1, self.depth):
            self.out3(k).wait_send()
            self.out4(k).wait_send()
        self.out5().wait_send()


def part_scratch(width, depth):
    block, thin = (TALL, width), (16, width)
    dma = pltpu.SemaphoreType.DMA
    return [
        pltpu.VMEM((3, 4, *block), BF16),
        pltpu.VMEM((3, 4, *block), BF16),
        pltpu.VMEM((3, *block), BF16),
        pltpu.VMEM((3, *block), BF16),
        pltpu.VMEM((depth * 16, width), F32),
        pltpu.VMEM((depth, *thin), BF16),
        pltpu.VMEM((depth - 1, *thin), BF16),
        pltpu.VMEM(thin, BF16),
        pltpu.VMEM((depth - 1, *thin), BF16),
        pltpu.VMEM((depth, *thin), BF16),
        pltpu.VMEM((depth, *thin), BF16),
        pltpu.VMEM((depth * 16, width), F32),
        dma((3, 4)), dma((3, 4)),
        dma((3,)), dma((3,)),
        dma((depth - 1,)), dma((depth - 1,)),
        dma((depth - 1,)), dma((depth - 1,)),
        dma, dma,
    ]


def layer_kernel(
    holders, depth,
    count_ref, table_ref, src_ref, tgt_ref, rot_ref, len_ref, turns_ref, grads_ref, feats_ref, radial_ref, w_hbm,
    node_ref, out_ref,
    turn_ref, rows_ref, packed_ref, meta_out, meta_in, grad_out, grad_in, w_ref,
    grad_ref, in_ref, pick_ref, scale_ref, acc_ref, own_ref, in_peer, grad_peer, half_in,
    ws, ms, mr, gs, gr, is_, ir, hs, hr, *sums,
):
    me, layer = lax.axis_index("graph"), lax.axis_index("dp")
    core, place = lax.rem(me, 2), me // 2
    x, y = place // 4, lax.rem(place, 4)
    rows = holders * CAP
    first = (1 - core) * x + core * y
    second = (1 - core) * y + core * x

    def chip(kind, a, b):
        return (1 - kind) * (a * 4 + b) + kind * (b * 4 + a)

    def index(a, b, c):
        return chip(core, lax.rem(first + a, 4), lax.rem(second + b, 4)) * 2 + lax.rem(core + c, 2)

    def along(a, b):
        return {"graph": index(a, b, 0)}

    partner = {"graph": index(0, 0, 1)}

    def above(k):
        return {"dp": lax.rem(layer + k, depth)}

    def remote(src, dst, ss, rs, peer):
        return pltpu.make_async_remote_copy(
            src_ref=src, dst_ref=dst, send_sem=ss, recv_sem=rs, device_id=peer, device_id_type=MESH
        )

    load_w = pltpu.make_async_copy(w_hbm, w_ref, ws)
    load_w.start()
    barrier = pltpu.get_barrier_semaphore()
    for a, b, c in STEPS:
        pl.semaphore_signal(barrier, inc=1, device_id={"graph": index(a, b, c)}, device_id_type=MESH)
    for k in range(1, depth):
        pl.semaphore_signal(barrier, inc=1, device_id=above(k), device_id_type=MESH)

    meta = find_meta(
        holders, count_ref, table_ref, src_ref, tgt_ref, rot_ref, len_ref, turns_ref, turn_ref, rows_ref
    )
    meta_out[...] = meta.reshape(holders, CAP, META).astype(BF16)
    pl.semaphore_wait(barrier, len(STEPS) + depth - 1)

    def meta_copy(k):
        peer = index(*STEPS[k - 1])
        return remote(meta_out.at[peer], meta_in.at[k], ms.at[k], mr.at[k], {"graph": peer})

    def grad_copy(k):
        peer = index(*STEPS[k - 1])
        return remote(grad_out.at[peer], grad_in.at[k], gs.at[k], gr.at[k], {"graph": peer})

    for k in range(1, holders):
        meta_copy(k).start()
    pack_nodes(grads_ref, packed_ref)
    pick = selector(meta, 50)
    position = iota((SPAN, CH), 0) & 63
    for degree in range(DEG):
        part = jnp.where(in_degree(position, degree), packed_ref[...], 0.0).astype(BF16)
        grad = dot(pick, part)
        grad_out[:, :, degree * CH : (degree + 1) * CH] = grad.reshape(holders, CAP, CH).astype(BF16)
    for k in range(1, holders):
        grad_copy(k).start()
    meta_in[0] = meta_out[me]
    grad_in[0] = grad_out[me]

    for k in range(1, holders):
        meta_copy(k).wait_recv()
    meta = meta_in[...].astype(F32).reshape(rows, META)
    lane = iota((rows, META), 1)
    length = jnp.sum(jnp.where((lane >= 52) & (lane < 55), meta, 0.0), axis=1, keepdims=True)
    live = meta[:, 51:52]
    gauss = radial_ref.shape[0]
    spacing = CUTOFF / (gauss - 1)
    centers = iota((1, gauss), 1).astype(F32) * spacing
    basis = jnp.exp((-0.5 / (2.0 * spacing) ** 2) * (length - centers) ** 2)
    scale_ref[...] = live * lax.dot_general(
        basis, radial_ref[...], (((1,), (0,)), ((), ())),
        precision=lax.Precision.HIGHEST, preferred_element_type=F32,
    )
    pick = selector(meta, 49)
    pick_ref[...] = pick.astype(F32).T.astype(BF16)
    pack_nodes(feats_ref, packed_ref)
    for degree in range(DEG):
        part = jnp.where(in_degree(position, degree), packed_ref[...], 0.0).astype(BF16)
        edge_in = dot(pick, part) * scale_ref[...]
        in_ref[degree * CH : (degree + 1) * CH, :] = edge_in.T.astype(BF16)
    acc_ref[...] = jnp.zeros(acc_ref.shape, F32)

    def columns(kind):
        return pl.ds(pl.multiple_of(kind * HALF, 128), HALF)

    in_copy = remote(in_ref, in_peer, is_, ir, partner)
    in_copy.start()

    def half_copy(n):
        slabs = pl.ds(GROUPS[n][0], GROUPS[n][1] - GROUPS[n][0])
        return remote(
            grad_in.at[slabs, :, columns(1 - core)], half_in.at[slabs], hs.at[n], hr.at[n], partner
        )

    def arrive(n):
        begin, end = GROUPS[n]
        for k in range(max(begin, 1), end):
            grad_copy(k).wait_recv()
        half_copy(n).start()
        for degree in range(DEG):
            cols = slice(degree * CH, (degree + 1) * CH)
            slab = grad_in[begin:end, :, cols].astype(F32)
            grad_ref[begin * CAP : end * CAP, cols] = slab.reshape(-1, CH).astype(BF16)

    def arrive_peer(n):
        begin, end = GROUPS[n]
        half_copy(n).wait_recv()
        for at, width in PARTS:
            slab = half_in[begin:end, :, at : at + width].astype(F32)
            grad_peer[begin * CAP : end * CAP, at : at + width] = slab.reshape(-1, width).astype(BF16)

    def weights(p):
        cols = pl.ds(pl.multiple_of(core * HALF + p.at, 128), p.width)

        def terms(t, _):
            tall = pl.ds(pl.multiple_of(t * (WIDTH // 2), 128), WIDTH // 2)
            term = dot(in_ref[tall, :], grad_ref[:, cols])
            term += dot(in_peer[tall, :], grad_peer[:, p.at : p.at + p.width])
            own_ref[tall, p.at : p.at + p.width] = term
            return 0

        lax.fori_loop(0, 2, terms, 0)

    def backward(degree, _):
        at = pl.ds(pl.multiple_of(degree * CH, CH), CH)
        hidden = dot(grad_ref[...], w_ref[at, :], ((1,), (1,)))
        back = (hidden * scale_ref[...]).astype(BF16)
        term = dot(pick_ref[...], back)
        acc_ref[...] += jnp.where(in_degree(position, degree), term, 0.0)
        return 0

    for n in range(len(GROUPS)):
        arrive(n)
    in_copy.wait_recv()
    for n in range(len(GROUPS)):
        arrive_peer(n)
    each = len(sums) // len(PARTS)
    parts = [
        PartSum(at, width, own_ref, remote, along, above, layer, depth, partner, first, second, core,
                sums[n * each : (n + 1) * each])
        for n, (at, width) in enumerate(PARTS)
    ]
    for p in parts:
        weights(p)
        p.begin()
    load_w.wait()
    lax.fori_loop(0, 4, backward, 0)
    parts[0].second_axis()
    lax.fori_loop(4, DEG, backward, 0)
    for q in range(ROWS):
        node_ref[q] = acc_ref[q * 64 : q * 64 + COEF, :]
    stages = ("second_axis", "over_layers", "share", "trade")
    for wave in range(1, len(stages) + len(parts) - 1):
        for n, p in enumerate(parts):
            if 0 <= wave - n < len(stages):
                getattr(p, stages[wave - n])()
    for p in parts:
        p.finish(out_ref)

    for k in range(1, holders):
        meta_copy(k).wait_send()
        grad_copy(k).wait_send()
    in_copy.wait_send()
    for n in range(len(GROUPS)):
        half_copy(n).wait_send()
    for p in parts:
        p.sent()


def per_device(
    node_feats, node_grads, node_row, edge_src, edge_tgt, edge_rot, edge_len, edge_count, rotations, w_zero, w_radial,
    holders, depth,
):
    slots = edge_src.shape[1]
    turns = rotations.transpose(1, 2, 0)
    rows = holders * CAP
    vmem = pl.BlockSpec(memory_space=pltpu.VMEM)
    dma = pltpu.SemaphoreType.DMA
    buffer = pltpu.VMEM
    node, weight = pl.pallas_call(
        functools.partial(layer_kernel, holders, depth),
        out_shape=(
            jax.ShapeDtypeStruct((ROWS, COEF, CH), F32),
            jax.ShapeDtypeStruct((WIDTH // holders, WIDTH), F32),
        ),
        in_specs=[pl.BlockSpec(memory_space=pltpu.SMEM)] + [vmem] * 9 + [pl.BlockSpec(memory_space=pl.ANY)],
        out_specs=(vmem, vmem),
        scratch_shapes=[
            buffer((COEF, turns.shape[2]), BF16),
            buffer((META, slots), F32),
            buffer((SPAN, CH), F32),
            buffer((holders, CAP, META), BF16),
            buffer((holders, CAP, META), BF16),
            buffer((holders, CAP, WIDTH), BF16),
            buffer((holders, CAP, WIDTH), BF16),
            buffer((WIDTH, WIDTH), BF16),
            buffer((rows, WIDTH), BF16),
            buffer((WIDTH, rows), BF16),
            buffer((SPAN, rows), BF16),
            buffer((rows, CH), F32),
            buffer((SPAN, CH), F32),
            buffer((WIDTH, HALF), F32),
            buffer((WIDTH, rows), BF16),
            buffer((rows, HALF), BF16),
            buffer((holders, CAP, HALF), BF16),
            dma,
            dma((holders,)), dma((holders,)),
            dma((holders,)), dma((holders,)),
            dma, dma,
            dma((len(GROUPS),)), dma((len(GROUPS),)),
            *(shape for _, width in PARTS for shape in part_scratch(width, depth)),
        ],
        compiler_params=pltpu.CompilerParams(
            collective_id=0, has_side_effects=True, vmem_limit_bytes=VMEM_LIMIT
        ),
        name="layer",
    )(
        edge_count, node_row, edge_src, edge_tgt, edge_rot, edge_len, turns,
        node_grads[0], node_feats[0], w_radial, w_zero,
    )
    return (node[None], weight)


def solution(mesh):
    graph = P("dp", "graph")
    placed = (
        P("dp", "graph", None, None), P("dp", "graph", None, None), P("dp", None),
        graph, graph, graph, graph, graph, P(), P(), P(),
    )
    return jax.shard_map(
        functools.partial(per_device, holders=mesh.shape["graph"], depth=mesh.shape["dp"]),
        mesh=mesh,
        in_specs=placed,
        out_specs=(P("dp", "graph", None, None), P("graph", None)),
        check_vma=False,
    )
```

```python
import functools

import jax
import jax.numpy as jnp
from jax import lax
from jax.experimental import pallas as pl
from jax.experimental.pallas import tpu as pltpu
from jax.sharding import PartitionSpec as P

CUTOFF = 12.0
CAP = 24
DEG = 7
COEF = 49
ROWS = 7
CH = 256
WIDTH = DEG * CH
META = 128
HALF = WIDTH // 2
TALL = 112
PARTS = ((0, 384), (384, 512))
SPAN = 64 * ROWS
F32, BF16, I32 = jnp.float32, jnp.bfloat16, jnp.int32
MESH = pl.DeviceIdType.MESH
VMEM_LIMIT = 60 * 1024 * 1024
FAR = (
    (2, 2), (2, 1), (1, 2), (2, 3), (3, 2), (2, 0), (0, 2), (1, 1),
    (3, 3), (1, 3), (3, 1), (1, 0), (0, 1), (3, 0), (0, 3),
)
GROUPS = ((0, 16), (16, 26), (26, 32))
STEPS = [(a, b, c) for c in (0, 1) for a, b in FAR] + [(0, 0, 1)]


def iota(shape, dim):
    return lax.broadcasted_iota(I32, shape, dim)


def onehot(mask):
    return jnp.where(mask, 1.0, 0.0).astype(BF16)


def dot(a, b, dims=((1,), (0,))):
    return lax.dot_general(a, b, (dims, ((), ())), preferred_element_type=F32)


def spread_matrix():
    j, lane = iota((META, SPAN), 0), iota((META, SPAN), 1)
    return onehot((lane & 63 == j) & (j < COEF))


def selector(meta, column):
    wide = dot(meta.astype(BF16), spread_matrix())
    atom = meta[:, column : column + 1].astype(I32)
    return jnp.where(iota(wide.shape, 1) >> 6 == atom, wide, 0.0).astype(BF16)


def in_degree(position, degree):
    return (position >= degree * degree) & (position < (degree + 1) * (degree + 1))


def pack_nodes(nodes_ref, packed_ref):
    packed_ref[...] = jnp.zeros(packed_ref.shape, F32)
    for q in range(ROWS):
        packed_ref[q * 64 : q * 64 + COEF, :] = nodes_ref[q].astype(F32)


def find_meta(holders, count_ref, table_ref, src_ref, tgt_ref, rot_ref, len_ref, turns_ref, turn_ref, rows_ref):
    own = lax.axis_index("graph")
    slots = src_ref.shape[1]
    atoms = table_ref.shape[1]
    live = iota((1, slots), 1) < count_ref[0, 0]
    table = jnp.broadcast_to(table_ref[...].astype(F32), (8, atoms)).astype(BF16)

    def rows_of(ids):
        return dot(table, onehot(iota((atoms, slots), 0) == ids))[0:1].astype(I32)

    src = rows_of(src_ref[...])
    tgt = rows_of(tgt_ref[...])
    holder = (src * 9363) >> 16
    held = onehot((iota((holders, slots), 0) == holder) & live)
    before = onehot(iota((slots, slots), 0) < iota((slots, slots), 1))
    rank = jnp.sum(held.astype(F32) * dot(held, before), axis=0, keepdims=True)
    place = jnp.where(live, holder * CAP + rank.astype(I32), -1)
    chosen = onehot(iota((holders * CAP, slots), 0) == place)

    total = turns_ref[0].astype(F32)
    for degree in range(1, DEG):
        total += turns_ref[degree].astype(F32)
    turn_ref[...] = total.astype(BF16)
    step = 512
    turned = jnp.zeros((COEF, slots), F32)
    for start in range(0, turns_ref.shape[2], step):
        turned += dot(
            turn_ref[:, start : start + step],
            onehot(iota((step, slots), 0) + start == rot_ref[...]),
        )
    length = len_ref[...]
    high = length.astype(BF16).astype(F32)
    middle = (length - high).astype(BF16).astype(F32)
    rows_ref[...] = jnp.zeros(rows_ref.shape, F32)
    rows_ref[0:COEF, :] = turned
    rows_ref[49:50, :] = (src - holder * ROWS).astype(F32)
    rows_ref[50:51, :] = (tgt - own * ROWS).astype(F32)
    rows_ref[51:52, :] = jnp.ones((1, slots), F32)
    rows_ref[52:53, :] = high
    rows_ref[53:54, :] = middle
    rows_ref[54:55, :] = length - high - middle
    return dot(chosen, rows_ref[...].astype(BF16), ((1,), (1,)))


class PartSum:
    def __init__(self, at, width, own, remote, along, above, layer, depth, partner, site, first, second, core, refs):
        self.at, self.width, self.own, self.remote, self.along, self.above = at, width, own, remote, along, above
        self.site = site
        self.layer, self.depth, self.partner, self.first, self.second, self.core = (
            layer, depth, partner, first, second, core
        )
        (
            self.send1, self.recv1, self.send2, self.recv2, self.total, self.send3, self.recv3,
            self.mine, self.recv4, self.held,
            self.s1, self.r1, self.s2, self.r2, self.s3, self.r3, self.s4, self.r4,
        ) = refs

    def block(self, k, m):
        a, b = lax.rem(self.first + k, 4), lax.rem(self.second + m, 4)
        place = (1 - self.core) * (a * 4 + b) + self.core * (b * 4 + a)
        return self.own[pl.ds(pl.multiple_of(place * TALL, 16), TALL), self.at : self.at + self.width]

    def out1(self, i, k):
        to = k if k != 2 else 1 if i < 2 else 3
        return self.remote(
            self.send1.at[k - 1, i], self.recv1.at[k - 1, i], self.s1.at[k - 1, i], self.r1.at[k - 1, i],
            self.along(to, 0),
        )

    def out2(self, m):
        return self.remote(
            self.send2.at[m - 1], self.recv2.at[m - 1], self.s2.at[m - 1], self.r2.at[m - 1], self.along(0, m)
        )

    def out3(self, k):
        to = lax.rem(self.layer + k, self.depth)
        return self.remote(
            self.send3.at[to], self.recv3.at[k - 1], self.s3.at[k - 1], self.r3.at[k - 1], self.above(k)
        )

    def out4(self, k):
        half = self.depth // 2
        slot = lax.rem(self.layer, half)
        return self.remote(
            self.mine, self.recv4.at[self.core, slot], self.s4.at[k], self.r4.at[self.core, slot],
            {"graph": self.site + self.layer // half, "dp": lax.rem(self.layer + k, self.depth)},
        )

    def is_holder(self):
        return self.layer // (self.depth // 2) == self.core

    def turns(self):
        return sorted(range(1, self.depth), key=lambda k: (-min(k, self.depth - k), k))

    def begin(self):
        for k, i in ((2, 0), (2, 2), (2, 1), (2, 3), (1, 2), (3, 0), (1, 3), (3, 1)):
            self.send1[k - 1, i] = self.block(k, i + 1).astype(BF16)
            self.out1(i, k).start()

    def merge(self):
        for k, i in ((1, 0), (3, 2), (1, 1), (3, 3)):
            self.out1(i, 2).wait_recv()
            self.send1[k - 1, i] = (self.block(k, i + 1) + self.recv1[1, i].astype(F32)).astype(BF16)
            self.out1(i, k).start()

    def gathered(self, i):
        got = self.block(0, i + 1)
        for k in (1, 3):
            self.out1(i, k).wait_recv()
            got += self.recv1[k - 1, i].astype(F32)
        return got

    def second_axis(self):
        for m in (1, 3, 2):
            self.send2[m - 1] = self.gathered(m - 1).astype(BF16)
            self.out2(m).start()
        self.held[...] = self.gathered(3)

    def over_layers(self):
        kept = self.held[...]
        for m in (1, 2, 3):
            self.out2(m).wait_recv()
            kept += self.recv2[m - 1].astype(F32)
        half, mid = TALL // 2, self.total.shape[0] // 2
        self.total[...] = jnp.zeros(self.total.shape, F32)
        self.total[0:half, :] = kept[0:half]
        self.total[mid : mid + half, :] = kept[half:]
        self.send3[...] = self.total[...].astype(BF16).reshape(self.send3.shape)
        for k in self.turns():
            self.out3(k).start()

    def share(self):
        part = self.total[pl.ds(pl.multiple_of(self.layer * 16, 16), 16), :]
        for k in range(1, self.depth):
            self.out3(k).wait_recv()
            part += self.recv3[k - 1].astype(F32)
        self.mine[...] = part.astype(BF16)
        for k in self.turns():
            self.out4(k).start()

        @pl.when(jnp.logical_not(self.is_holder()))
        def _():
            self.out4(0).start()

        @pl.when(self.is_holder())
        def _():
            self.recv4[self.core, lax.rem(self.layer, self.depth // 2)] = self.mine[...]

    def finish(self, out_ref):
        half = self.depth // 2
        for kind in (0, 1):
            for slot in range(half):
                here = (self.core * half + slot == self.layer) & (self.core == kind)

                @pl.when(jnp.logical_not(here))
                def _(kind=kind, slot=slot):
                    self.remote(
                        self.mine, self.recv4.at[kind, slot], self.s4.at[0], self.r4.at[kind, slot], self.partner
                    ).wait_recv()

                tall = min(16, out_ref.shape[0] - slot * 16)
                at = kind * HALF + self.at
                rows = self.recv4[kind, slot].astype(F32)
                out_ref[slot * 16 : slot * 16 + tall, at : at + self.width] = rows[0:tall]

    def sent(self):
        for k in (1, 2, 3):
            for i in range(4):
                self.out1(i, k).wait_send()
            self.out2(k).wait_send()
        for k in range(1, self.depth):
            self.out3(k).wait_send()
            self.out4(k).wait_send()

        @pl.when(jnp.logical_not(self.is_holder()))
        def _():
            self.out4(0).wait_send()


def part_scratch(width, depth):
    block, thin = (TALL, width), (16, width)
    dma = pltpu.SemaphoreType.DMA
    return [
        pltpu.VMEM((3, 4, *block), BF16),
        pltpu.VMEM((3, 4, *block), BF16),
        pltpu.VMEM((3, *block), BF16),
        pltpu.VMEM((3, *block), BF16),
        pltpu.VMEM((depth * 16, width), F32),
        pltpu.VMEM((depth, *thin), BF16),
        pltpu.VMEM((depth - 1, *thin), BF16),
        pltpu.VMEM(thin, BF16),
        pltpu.VMEM((2, depth // 2, *thin), BF16),
        pltpu.VMEM(block, F32),
        dma((3, 4)), dma((3, 4)),
        dma((3,)), dma((3,)),
        dma((depth - 1,)), dma((depth - 1,)),
        dma((depth,)), dma((2, depth // 2)),
    ]


def layer_kernel(
    holders, depth,
    count_ref, table_ref, src_ref, tgt_ref, rot_ref, len_ref, turns_ref, grads_ref, feats_ref, radial_ref, w_hbm,
    node_ref, out_ref,
    turn_ref, rows_ref, packed_ref, meta_out, meta_in, grad_out, grad_in, w_ref,
    grad_ref, in_ref, pick_ref, scale_ref, acc_ref, own_ref, in_peer, grad_peer, half_in,
    ws, ms, mr, gs, gr, is_, ir, hs, hr, *sums,
):
    me, layer = lax.axis_index("graph"), lax.axis_index("dp")
    core, place = lax.rem(me, 2), me // 2
    x, y = place // 4, lax.rem(place, 4)
    rows = holders * CAP
    first = (1 - core) * x + core * y
    second = (1 - core) * y + core * x

    def chip(kind, a, b):
        return (1 - kind) * (a * 4 + b) + kind * (b * 4 + a)

    def index(a, b, c):
        return chip(core, lax.rem(first + a, 4), lax.rem(second + b, 4)) * 2 + lax.rem(core + c, 2)

    def along(a, b):
        return {"graph": index(a, b, 0)}

    partner = {"graph": index(0, 0, 1)}

    def above(k):
        return {"dp": lax.rem(layer + k, depth)}

    def remote(src, dst, ss, rs, peer):
        return pltpu.make_async_remote_copy(
            src_ref=src, dst_ref=dst, send_sem=ss, recv_sem=rs, device_id=peer, device_id_type=MESH
        )

    load_w = pltpu.make_async_copy(w_hbm, w_ref, ws)
    load_w.start()
    barrier = pltpu.get_barrier_semaphore()
    for a, b, c in STEPS:
        pl.semaphore_signal(barrier, inc=1, device_id={"graph": index(a, b, c)}, device_id_type=MESH)
    for k in range(1, depth):
        pl.semaphore_signal(barrier, inc=1, device_id=above(k), device_id_type=MESH)
        pl.semaphore_signal(barrier, inc=1, device_id={**partner, **above(k)}, device_id_type=MESH)

    meta = find_meta(
        holders, count_ref, table_ref, src_ref, tgt_ref, rot_ref, len_ref, turns_ref, turn_ref, rows_ref
    )
    meta_out[...] = meta.reshape(holders, CAP, META).astype(BF16)
    pl.semaphore_wait(barrier, len(STEPS) + 2 * (depth - 1))

    def meta_copy(k):
        peer = index(*STEPS[k - 1])
        return remote(meta_out.at[peer], meta_in.at[k], ms.at[k], mr.at[k], {"graph": peer})

    def grad_copy(k):
        peer = index(*STEPS[k - 1])
        return remote(grad_out.at[peer], grad_in.at[k], gs.at[k], gr.at[k], {"graph": peer})

    for k in range(1, holders):
        meta_copy(k).start()
    pack_nodes(grads_ref, packed_ref)
    pick = selector(meta, 50)
    position = iota((SPAN, CH), 0) & 63
    for degree in range(DEG):
        part = jnp.where(in_degree(position, degree), packed_ref[...], 0.0).astype(BF16)
        grad = dot(pick, part)
        grad_out[:, :, degree * CH : (degree + 1) * CH] = grad.reshape(holders, CAP, CH).astype(BF16)
    for k in range(1, holders):
        grad_copy(k).start()
    meta_in[0] = meta_out[me]
    grad_in[0] = grad_out[me]

    for k in range(1, holders):
        meta_copy(k).wait_recv()
    meta = meta_in[...].astype(F32).reshape(rows, META)
    lane = iota((rows, META), 1)
    length = jnp.sum(jnp.where((lane >= 52) & (lane < 55), meta, 0.0), axis=1, keepdims=True)
    live = meta[:, 51:52]
    gauss = radial_ref.shape[0]
    spacing = CUTOFF / (gauss - 1)
    centers = iota((1, gauss), 1).astype(F32) * spacing
    basis = jnp.exp((-0.5 / (2.0 * spacing) ** 2) * (length - centers) ** 2)
    scale_ref[...] = live * lax.dot_general(
        basis, radial_ref[...], (((1,), (0,)), ((), ())),
        precision=lax.Precision.HIGHEST, preferred_element_type=F32,
    )
    pick = selector(meta, 49)
    pick_ref[...] = pick.astype(F32).T.astype(BF16)
    pack_nodes(feats_ref, packed_ref)
    for degree in range(DEG):
        part = jnp.where(in_degree(position, degree), packed_ref[...], 0.0).astype(BF16)
        edge_in = dot(pick, part) * scale_ref[...]
        in_ref[degree * CH : (degree + 1) * CH, :] = edge_in.T.astype(BF16)
    acc_ref[...] = jnp.zeros(acc_ref.shape, F32)

    def columns(kind):
        return pl.ds(pl.multiple_of(kind * HALF, 128), HALF)

    in_copy = remote(in_ref, in_peer, is_, ir, partner)
    in_copy.start()

    def half_copy(n):
        slabs = pl.ds(GROUPS[n][0], GROUPS[n][1] - GROUPS[n][0])
        return remote(
            grad_in.at[slabs, :, columns(1 - core)], half_in.at[slabs], hs.at[n], hr.at[n], partner
        )

    def arrive(n):
        begin, end = GROUPS[n]
        for k in range(max(begin, 1), end):
            grad_copy(k).wait_recv()
        half_copy(n).start()
        for degree in range(DEG):
            cols = slice(degree * CH, (degree + 1) * CH)
            slab = grad_in[begin:end, :, cols].astype(F32)
            grad_ref[begin * CAP : end * CAP, cols] = slab.reshape(-1, CH).astype(BF16)

    def arrive_peer(n):
        begin, end = GROUPS[n]
        half_copy(n).wait_recv()
        for at, width in PARTS:
            slab = half_in[begin:end, :, at : at + width].astype(F32)
            grad_peer[begin * CAP : end * CAP, at : at + width] = slab.reshape(-1, width).astype(BF16)

    def weights(p):
        cols = pl.ds(pl.multiple_of(core * HALF + p.at, 128), p.width)

        def terms(t, _):
            tall = pl.ds(pl.multiple_of(t * (WIDTH // 2), 128), WIDTH // 2)
            term = dot(in_ref[tall, :], grad_ref[:, cols])
            term += dot(in_peer[tall, :], grad_peer[:, p.at : p.at + p.width])
            own_ref[tall, p.at : p.at + p.width] = term
            return 0

        lax.fori_loop(0, 2, terms, 0)

    def backward(degree, _):
        at = pl.ds(pl.multiple_of(degree * CH, CH), CH)
        hidden = dot(grad_ref[...], w_ref[at, :], ((1,), (1,)))
        back = (hidden * scale_ref[...]).astype(BF16)
        term = dot(pick_ref[...], back)
        acc_ref[...] += jnp.where(in_degree(position, degree), term, 0.0)
        return 0

    for n in range(len(GROUPS)):
        arrive(n)
    in_copy.wait_recv()
    for n in range(len(GROUPS)):
        arrive_peer(n)
    each = len(sums) // len(PARTS)
    parts = [
        PartSum(at, width, own_ref, remote, along, above, layer, depth, partner, place * 2, first, second, core,
                sums[n * each : (n + 1) * each])
        for n, (at, width) in enumerate(PARTS)
    ]
    for p in parts:
        weights(p)
        p.begin()
    parts[0].merge()
    load_w.wait()
    lax.fori_loop(0, 3, backward, 0)
    parts[1].merge()
    lax.fori_loop(3, 5, backward, 0)
    parts[0].second_axis()
    lax.fori_loop(5, DEG, backward, 0)
    for q in range(ROWS):
        node_ref[q] = acc_ref[q * 64 : q * 64 + COEF, :]
    parts[0].over_layers()
    parts[1].second_axis()
    parts[0].share()
    parts[1].over_layers()
    parts[1].share()
    for p in parts:
        p.finish(out_ref)

    for k in range(1, holders):
        meta_copy(k).wait_send()
        grad_copy(k).wait_send()
    in_copy.wait_send()
    for n in range(len(GROUPS)):
        half_copy(n).wait_send()
    for p in parts:
        p.sent()


def per_device(
    node_feats, node_grads, node_row, edge_src, edge_tgt, edge_rot, edge_len, edge_count, rotations, w_zero, w_radial,
    holders, depth,
):
    slots = edge_src.shape[1]
    turns = rotations.transpose(1, 2, 0)
    rows = holders * CAP
    vmem = pl.BlockSpec(memory_space=pltpu.VMEM)
    dma = pltpu.SemaphoreType.DMA
    buffer = pltpu.VMEM
    node, weight = pl.pallas_call(
        functools.partial(layer_kernel, holders, depth),
        out_shape=(
            jax.ShapeDtypeStruct((ROWS, COEF, CH), F32),
            jax.ShapeDtypeStruct((WIDTH // holders, WIDTH), F32),
        ),
        in_specs=[pl.BlockSpec(memory_space=pltpu.SMEM)] + [vmem] * 9 + [pl.BlockSpec(memory_space=pl.ANY)],
        out_specs=(vmem, vmem),
        scratch_shapes=[
            buffer((COEF, turns.shape[2]), BF16),
            buffer((META, slots), F32),
            buffer((SPAN, CH), F32),
            buffer((holders, CAP, META), BF16),
            buffer((holders, CAP, META), BF16),
            buffer((holders, CAP, WIDTH), BF16),
            buffer((holders, CAP, WIDTH), BF16),
            buffer((WIDTH, WIDTH), BF16),
            buffer((rows, WIDTH), BF16),
            buffer((WIDTH, rows), BF16),
            buffer((SPAN, rows), BF16),
            buffer((rows, CH), F32),
            buffer((SPAN, CH), F32),
            buffer((WIDTH, HALF), F32),
            buffer((WIDTH, rows), BF16),
            buffer((rows, HALF), BF16),
            buffer((holders, CAP, HALF), BF16),
            dma,
            dma((holders,)), dma((holders,)),
            dma((holders,)), dma((holders,)),
            dma, dma,
            dma((len(GROUPS),)), dma((len(GROUPS),)),
            *(shape for _, width in PARTS for shape in part_scratch(width, depth)),
        ],
        compiler_params=pltpu.CompilerParams(
            collective_id=0, has_side_effects=True, vmem_limit_bytes=VMEM_LIMIT
        ),
        name="layer",
    )(
        edge_count, node_row, edge_src, edge_tgt, edge_rot, edge_len, turns,
        node_grads[0], node_feats[0], w_radial, w_zero,
    )
    return (node[None], weight)


def solution(mesh):
    graph = P("dp", "graph")
    placed = (
        P("dp", "graph", None, None), P("dp", "graph", None, None), P("dp", None),
        graph, graph, graph, graph, graph, P(), P(), P(),
    )
    return jax.shard_map(
        functools.partial(per_device, holders=mesh.shape["graph"], depth=mesh.shape["dp"]),
        mesh=mesh,
        in_specs=placed,
        out_specs=(P("dp", "graph", None, None), P("graph", None)),
        check_vma=False,
    )
```

```python
import functools

import jax
import jax.numpy as jnp
from jax import lax
from jax.experimental import pallas as pl
from jax.experimental.pallas import tpu as pltpu
from jax.sharding import PartitionSpec as P

CUTOFF = 12.0
CAP = 24
DEG = 7
COEF = 49
ROWS = 7
CH = 256
WIDTH = DEG * CH
META = 128
HALF = WIDTH // 2
TALL = 112
PARTS = ((0, 384), (384, 512))
SPAN = 64 * ROWS
F32, BF16, I32 = jnp.float32, jnp.bfloat16, jnp.int32
MESH = pl.DeviceIdType.MESH
VMEM_LIMIT = 60 * 1024 * 1024
FAR = (
    (2, 2), (2, 1), (1, 2), (2, 3), (3, 2), (2, 0), (0, 2), (1, 1),
    (3, 3), (1, 3), (3, 1), (1, 0), (0, 1), (3, 0), (0, 3),
)
GROUPS = ((0, 16), (16, 26), (26, 32))
STEPS = [(a, b, c) for c in (0, 1) for a, b in FAR] + [(0, 0, 1)]


def iota(shape, dim):
    return lax.broadcasted_iota(I32, shape, dim)


def onehot(mask):
    return jnp.where(mask, 1.0, 0.0).astype(BF16)


def dot(a, b, dims=((1,), (0,))):
    return lax.dot_general(a, b, (dims, ((), ())), preferred_element_type=F32)


def spread_matrix():
    j, lane = iota((META, SPAN), 0), iota((META, SPAN), 1)
    return onehot((lane & 63 == j) & (j < COEF))


def selector(meta, column):
    wide = dot(meta.astype(BF16), spread_matrix())
    atom = meta[:, column : column + 1].astype(I32)
    return jnp.where(iota(wide.shape, 1) >> 6 == atom, wide, 0.0).astype(BF16)


def in_degree(position, degree):
    return (position >= degree * degree) & (position < (degree + 1) * (degree + 1))


def pack_nodes(nodes_ref, packed_ref):
    packed_ref[...] = jnp.zeros(packed_ref.shape, F32)
    for q in range(ROWS):
        packed_ref[q * 64 : q * 64 + COEF, :] = nodes_ref[q].astype(F32)


def find_meta(holders, count_ref, table_ref, src_ref, tgt_ref, rot_ref, len_ref, turns_ref, turn_ref, rows_ref):
    own = lax.axis_index("graph")
    slots = src_ref.shape[1]
    atoms = table_ref.shape[1]
    live = iota((1, slots), 1) < count_ref[0, 0]
    table = jnp.broadcast_to(table_ref[...].astype(F32), (8, atoms)).astype(BF16)

    def rows_of(ids):
        return dot(table, onehot(iota((atoms, slots), 0) == ids))[0:1].astype(I32)

    src = rows_of(src_ref[...])
    tgt = rows_of(tgt_ref[...])
    holder = (src * 9363) >> 16
    held = onehot((iota((holders, slots), 0) == holder) & live)
    before = onehot(iota((slots, slots), 0) < iota((slots, slots), 1))
    rank = jnp.sum(held.astype(F32) * dot(held, before), axis=0, keepdims=True)
    place = jnp.where(live, holder * CAP + rank.astype(I32), -1)
    chosen = onehot(iota((holders * CAP, slots), 0) == place)

    total = turns_ref[0].astype(F32)
    for degree in range(1, DEG):
        total += turns_ref[degree].astype(F32)
    turn_ref[...] = total.astype(BF16)
    step = 512
    turned = jnp.zeros((COEF, slots), F32)
    for start in range(0, turns_ref.shape[2], step):
        turned += dot(
            turn_ref[:, start : start + step],
            onehot(iota((step, slots), 0) + start == rot_ref[...]),
        )
    length = len_ref[...]
    high = length.astype(BF16).astype(F32)
    middle = (length - high).astype(BF16).astype(F32)
    rows_ref[...] = jnp.zeros(rows_ref.shape, F32)
    rows_ref[0:COEF, :] = turned
    rows_ref[49:50, :] = (src - holder * ROWS).astype(F32)
    rows_ref[50:51, :] = (tgt - own * ROWS).astype(F32)
    rows_ref[51:52, :] = jnp.ones((1, slots), F32)
    rows_ref[52:53, :] = high
    rows_ref[53:54, :] = middle
    rows_ref[54:55, :] = length - high - middle
    return dot(chosen, rows_ref[...].astype(BF16), ((1,), (1,)))


class PartSum:
    def __init__(self, at, width, own, remote, along, above, layer, depth, partner, site, first, second, core, refs):
        self.at, self.width, self.own, self.remote, self.along, self.above = at, width, own, remote, along, above
        self.site = site
        self.layer, self.depth, self.partner, self.first, self.second, self.core = (
            layer, depth, partner, first, second, core
        )
        (
            self.send1, self.recv1, self.send2, self.recv2, self.total, self.send3, self.recv3,
            self.mine, self.recv4, self.held,
            self.s1, self.r1, self.s2, self.r2, self.s3, self.r3, self.s4, self.r4,
        ) = refs

    def block(self, k, m):
        a, b = lax.rem(self.first + k, 4), lax.rem(self.second + m, 4)
        place = (1 - self.core) * (a * 4 + b) + self.core * (b * 4 + a)
        return self.own[pl.ds(pl.multiple_of(place * TALL, 16), TALL), self.at : self.at + self.width]

    def out1(self, i, k):
        to = k if k != 2 else 1 if i < 2 else 3
        return self.remote(
            self.send1.at[k - 1, i], self.recv1.at[k - 1, i], self.s1.at[k - 1, i], self.r1.at[k - 1, i],
            self.along(to, 0),
        )

    def out2(self, m):
        return self.remote(
            self.send2.at[m - 1], self.recv2.at[m - 1], self.s2.at[m - 1], self.r2.at[m - 1], self.along(0, m)
        )

    def out3(self, k):
        to = lax.rem(self.layer + k, self.depth)
        return self.remote(
            self.send3.at[to], self.recv3.at[k - 1], self.s3.at[k - 1], self.r3.at[k - 1], self.above(k)
        )

    def out4(self, k):
        half = self.depth // 2
        slot = lax.rem(self.layer, half)
        return self.remote(
            self.mine, self.recv4.at[self.core, slot], self.s4.at[k], self.r4.at[self.core, slot],
            {"graph": self.site + self.layer // half, "dp": lax.rem(self.layer + k, self.depth)},
        )

    def is_holder(self):
        return self.layer // (self.depth // 2) == self.core

    def turns(self):
        return sorted(range(1, self.depth), key=lambda k: (-min(k, self.depth - k), k))

    def begin(self):
        for k, i in ((2, 0), (2, 2), (2, 1), (2, 3), (1, 2), (3, 0), (1, 3), (3, 1)):
            self.send1[k - 1, i] = self.block(k, i + 1).astype(BF16)
            self.out1(i, k).start()

    def merge(self):
        for k, i in ((1, 0), (3, 2), (1, 1), (3, 3)):
            self.out1(i, 2).wait_recv()
            self.send1[k - 1, i] = (self.block(k, i + 1) + self.recv1[1, i].astype(F32)).astype(BF16)
            self.out1(i, k).start()

    def gathered(self, i):
        got = self.block(0, i + 1)
        for k in (1, 3):
            self.out1(i, k).wait_recv()
            got += self.recv1[k - 1, i].astype(F32)
        return got

    def second_axis(self):
        for m in (1, 3, 2):
            self.send2[m - 1] = self.gathered(m - 1).astype(BF16)
            self.out2(m).start()
        self.held[...] = self.gathered(3)

    def over_layers(self):
        kept = self.held[...]
        for m in (1, 2, 3):
            self.out2(m).wait_recv()
            kept += self.recv2[m - 1].astype(F32)
        half, mid = TALL // 2, self.total.shape[0] // 2
        self.total[...] = jnp.zeros(self.total.shape, F32)
        self.total[0:half, :] = kept[0:half]
        self.total[mid : mid + half, :] = kept[half:]
        self.send3[...] = self.total[...].astype(BF16).reshape(self.send3.shape)
        for k in self.turns():
            self.out3(k).start()

    def share(self):
        part = self.total[pl.ds(pl.multiple_of(self.layer * 16, 16), 16), :]
        for k in range(1, self.depth):
            self.out3(k).wait_recv()
            part += self.recv3[k - 1].astype(F32)
        self.mine[...] = part.astype(BF16)
        for k in self.turns():
            self.out4(k).start()

        @pl.when(jnp.logical_not(self.is_holder()))
        def _():
            self.out4(0).start()

        @pl.when(self.is_holder())
        def _():
            self.recv4[self.core, lax.rem(self.layer, self.depth // 2)] = self.mine[...]

    def finish(self, out_ref):
        half = self.depth // 2
        for kind in (0, 1):
            for slot in range(half):
                here = (self.core * half + slot == self.layer) & (self.core == kind)

                @pl.when(jnp.logical_not(here))
                def _(kind=kind, slot=slot):
                    self.remote(
                        self.mine, self.recv4.at[kind, slot], self.s4.at[0], self.r4.at[kind, slot], self.partner
                    ).wait_recv()

                tall = min(16, out_ref.shape[0] - slot * 16)
                at = kind * HALF + self.at
                rows = self.recv4[kind, slot].astype(F32)
                out_ref[slot * 16 : slot * 16 + tall, at : at + self.width] = rows[0:tall]

    def sent_chips(self):
        for k in (1, 2, 3):
            for i in range(4):
                self.out1(i, k).wait_send()
            self.out2(k).wait_send()

    def sent_layers(self):
        for k in range(1, self.depth):
            self.out3(k).wait_send()

    def sent_holders(self):
        for k in range(1, self.depth):
            self.out4(k).wait_send()

        @pl.when(jnp.logical_not(self.is_holder()))
        def _():
            self.out4(0).wait_send()


def part_scratch(width, depth):
    block, thin = (TALL, width), (16, width)
    dma = pltpu.SemaphoreType.DMA
    return [
        pltpu.VMEM((3, 4, *block), BF16),
        pltpu.VMEM((3, 4, *block), BF16),
        pltpu.VMEM((3, *block), BF16),
        pltpu.VMEM((3, *block), BF16),
        pltpu.VMEM((depth * 16, width), F32),
        pltpu.VMEM((depth, *thin), BF16),
        pltpu.VMEM((depth - 1, *thin), BF16),
        pltpu.VMEM(thin, BF16),
        pltpu.VMEM((2, depth // 2, *thin), BF16),
        pltpu.VMEM(block, F32),
        dma((3, 4)), dma((3, 4)),
        dma((3,)), dma((3,)),
        dma((depth - 1,)), dma((depth - 1,)),
        dma((depth,)), dma((2, depth // 2)),
    ]


def layer_kernel(
    holders, depth,
    count_ref, table_ref, src_ref, tgt_ref, rot_ref, len_ref, turns_ref, grads_ref, feats_ref, radial_ref, w_hbm,
    node_ref, out_ref,
    turn_ref, rows_ref, packed_ref, meta_out, meta_in, grad_out, grad_in, w_ref,
    grad_ref, in_ref, pick_ref, scale_ref, acc_ref, own_ref, in_peer, grad_peer, half_in,
    ws, ms, mr, gs, gr, is_, ir, hs, hr, *sums,
):
    me, layer = lax.axis_index("graph"), lax.axis_index("dp")
    core, place = lax.rem(me, 2), me // 2
    x, y = place // 4, lax.rem(place, 4)
    rows = holders * CAP
    first = (1 - core) * x + core * y
    second = (1 - core) * y + core * x

    def chip(kind, a, b):
        return (1 - kind) * (a * 4 + b) + kind * (b * 4 + a)

    def index(a, b, c):
        return chip(core, lax.rem(first + a, 4), lax.rem(second + b, 4)) * 2 + lax.rem(core + c, 2)

    def along(a, b):
        return {"graph": index(a, b, 0)}

    partner = {"graph": index(0, 0, 1)}

    def above(k):
        return {"dp": lax.rem(layer + k, depth)}

    def remote(src, dst, ss, rs, peer):
        return pltpu.make_async_remote_copy(
            src_ref=src, dst_ref=dst, send_sem=ss, recv_sem=rs, device_id=peer, device_id_type=MESH
        )

    load_w = pltpu.make_async_copy(w_hbm, w_ref, ws)
    load_w.start()
    barrier = pltpu.get_barrier_semaphore()
    for a, b, c in STEPS:
        pl.semaphore_signal(barrier, inc=1, device_id={"graph": index(a, b, c)}, device_id_type=MESH)
    for k in range(1, depth):
        pl.semaphore_signal(barrier, inc=1, device_id=above(k), device_id_type=MESH)
        pl.semaphore_signal(barrier, inc=1, device_id={**partner, **above(k)}, device_id_type=MESH)

    meta = find_meta(
        holders, count_ref, table_ref, src_ref, tgt_ref, rot_ref, len_ref, turns_ref, turn_ref, rows_ref
    )
    meta_out[...] = meta.reshape(holders, CAP, META).astype(BF16)
    pl.semaphore_wait(barrier, len(STEPS) + 2 * (depth - 1))

    def meta_copy(k):
        peer = index(*STEPS[k - 1])
        return remote(meta_out.at[peer], meta_in.at[k], ms.at[k], mr.at[k], {"graph": peer})

    def grad_copy(k):
        peer = index(*STEPS[k - 1])
        return remote(grad_out.at[peer], grad_in.at[k], gs.at[k], gr.at[k], {"graph": peer})

    for k in range(1, holders):
        meta_copy(k).start()
    pack_nodes(grads_ref, packed_ref)
    pick = selector(meta, 50)
    position = iota((SPAN, CH), 0) & 63
    for degree in range(DEG):
        part = jnp.where(in_degree(position, degree), packed_ref[...], 0.0).astype(BF16)
        grad = dot(pick, part)
        grad_out[:, :, degree * CH : (degree + 1) * CH] = grad.reshape(holders, CAP, CH).astype(BF16)
    for k in range(1, holders):
        grad_copy(k).start()
    meta_in[0] = meta_out[me]
    grad_in[0] = grad_out[me]

    for k in range(1, holders):
        meta_copy(k).wait_recv()
    meta = meta_in[...].astype(F32).reshape(rows, META)
    lane = iota((rows, META), 1)
    length = jnp.sum(jnp.where((lane >= 52) & (lane < 55), meta, 0.0), axis=1, keepdims=True)
    live = meta[:, 51:52]
    gauss = radial_ref.shape[0]
    spacing = CUTOFF / (gauss - 1)
    centers = iota((1, gauss), 1).astype(F32) * spacing
    basis = jnp.exp((-0.5 / (2.0 * spacing) ** 2) * (length - centers) ** 2)
    scale_ref[...] = live * lax.dot_general(
        basis, radial_ref[...], (((1,), (0,)), ((), ())),
        precision=lax.Precision.HIGHEST, preferred_element_type=F32,
    )
    pick = selector(meta, 49)
    pick_ref[...] = pick.astype(F32).T.astype(BF16)
    pack_nodes(feats_ref, packed_ref)
    for degree in range(DEG):
        part = jnp.where(in_degree(position, degree), packed_ref[...], 0.0).astype(BF16)
        edge_in = dot(pick, part) * scale_ref[...]
        in_ref[degree * CH : (degree + 1) * CH, :] = edge_in.T.astype(BF16)
    acc_ref[...] = jnp.zeros(acc_ref.shape, F32)

    def columns(kind):
        return pl.ds(pl.multiple_of(kind * HALF, 128), HALF)

    in_copy = remote(in_ref, in_peer, is_, ir, partner)
    in_copy.start()

    def half_copy(n):
        slabs = pl.ds(GROUPS[n][0], GROUPS[n][1] - GROUPS[n][0])
        return remote(
            grad_in.at[slabs, :, columns(1 - core)], half_in.at[slabs], hs.at[n], hr.at[n], partner
        )

    def arrive(n):
        begin, end = GROUPS[n]
        for k in range(max(begin, 1), end):
            grad_copy(k).wait_recv()
        half_copy(n).start()
        for degree in range(DEG):
            cols = slice(degree * CH, (degree + 1) * CH)
            slab = grad_in[begin:end, :, cols].astype(F32)
            grad_ref[begin * CAP : end * CAP, cols] = slab.reshape(-1, CH).astype(BF16)

    def arrive_peer(n):
        begin, end = GROUPS[n]
        half_copy(n).wait_recv()
        for at, width in PARTS:
            slab = half_in[begin:end, :, at : at + width].astype(F32)
            grad_peer[begin * CAP : end * CAP, at : at + width] = slab.reshape(-1, width).astype(BF16)

    def weights(p):
        cols = pl.ds(pl.multiple_of(core * HALF + p.at, 128), p.width)

        def terms(t, _):
            tall = pl.ds(pl.multiple_of(t * (WIDTH // 2), 128), WIDTH // 2)
            term = dot(in_ref[tall, :], grad_ref[:, cols])
            term += dot(in_peer[tall, :], grad_peer[:, p.at : p.at + p.width])
            own_ref[tall, p.at : p.at + p.width] = term
            return 0

        lax.fori_loop(0, 2, terms, 0)

    def backward(degree, _):
        at = pl.ds(pl.multiple_of(degree * CH, CH), CH)
        hidden = dot(grad_ref[...], w_ref[at, :], ((1,), (1,)))
        back = (hidden * scale_ref[...]).astype(BF16)
        term = dot(pick_ref[...], back)
        acc_ref[...] += jnp.where(in_degree(position, degree), term, 0.0)
        return 0

    for n in range(len(GROUPS)):
        arrive(n)
    in_copy.wait_recv()
    for n in range(len(GROUPS)):
        arrive_peer(n)
    each = len(sums) // len(PARTS)
    parts = [
        PartSum(at, width, own_ref, remote, along, above, layer, depth, partner, place * 2, first, second, core,
                sums[n * each : (n + 1) * each])
        for n, (at, width) in enumerate(PARTS)
    ]
    for p in parts:
        weights(p)
        p.begin()
    parts[0].merge()
    load_w.wait()
    lax.fori_loop(0, 3, backward, 0)
    parts[1].merge()
    lax.fori_loop(3, 5, backward, 0)
    parts[0].second_axis()
    lax.fori_loop(5, DEG, backward, 0)
    for q in range(ROWS):
        node_ref[q] = acc_ref[q * 64 : q * 64 + COEF, :]
    parts[0].over_layers()
    for k in range(1, holders):
        meta_copy(k).wait_send()
        grad_copy(k).wait_send()
    in_copy.wait_send()
    for n in range(len(GROUPS)):
        half_copy(n).wait_send()
    parts[1].second_axis()
    parts[0].share()
    parts[0].sent_chips()
    parts[1].over_layers()
    parts[0].sent_layers()
    parts[1].sent_chips()
    parts[0].finish(out_ref)
    parts[1].share()
    parts[0].sent_holders()
    parts[1].sent_layers()
    parts[1].finish(out_ref)
    parts[1].sent_holders()


def per_device(
    node_feats, node_grads, node_row, edge_src, edge_tgt, edge_rot, edge_len, edge_count, rotations, w_zero, w_radial,
    holders, depth,
):
    slots = edge_src.shape[1]
    turns = rotations.transpose(1, 2, 0)
    rows = holders * CAP
    vmem = pl.BlockSpec(memory_space=pltpu.VMEM)
    dma = pltpu.SemaphoreType.DMA
    buffer = pltpu.VMEM
    node, weight = pl.pallas_call(
        functools.partial(layer_kernel, holders, depth),
        out_shape=(
            jax.ShapeDtypeStruct((ROWS, COEF, CH), F32),
            jax.ShapeDtypeStruct((WIDTH // holders, WIDTH), F32),
        ),
        in_specs=[pl.BlockSpec(memory_space=pltpu.SMEM)] + [vmem] * 9 + [pl.BlockSpec(memory_space=pl.ANY)],
        out_specs=(vmem, vmem),
        scratch_shapes=[
            buffer((COEF, turns.shape[2]), BF16),
            buffer((META, slots), F32),
            buffer((SPAN, CH), F32),
            buffer((holders, CAP, META), BF16),
            buffer((holders, CAP, META), BF16),
            buffer((holders, CAP, WIDTH), BF16),
            buffer((holders, CAP, WIDTH), BF16),
            buffer((WIDTH, WIDTH), BF16),
            buffer((rows, WIDTH), BF16),
            buffer((WIDTH, rows), BF16),
            buffer((SPAN, rows), BF16),
            buffer((rows, CH), F32),
            buffer((SPAN, CH), F32),
            buffer((WIDTH, HALF), F32),
            buffer((WIDTH, rows), BF16),
            buffer((rows, HALF), BF16),
            buffer((holders, CAP, HALF), BF16),
            dma,
            dma((holders,)), dma((holders,)),
            dma((holders,)), dma((holders,)),
            dma, dma,
            dma((len(GROUPS),)), dma((len(GROUPS),)),
            *(shape for _, width in PARTS for shape in part_scratch(width, depth)),
        ],
        compiler_params=pltpu.CompilerParams(
            collective_id=0, has_side_effects=True, vmem_limit_bytes=VMEM_LIMIT
        ),
        name="layer",
    )(
        edge_count, node_row, edge_src, edge_tgt, edge_rot, edge_len, turns,
        node_grads[0], node_feats[0], w_radial, w_zero,
    )
    return (node[None], weight)


def solution(mesh):
    graph = P("dp", "graph")
    placed = (
        P("dp", "graph", None, None), P("dp", "graph", None, None), P("dp", None),
        graph, graph, graph, graph, graph, P(), P(), P(),
    )
    return jax.shard_map(
        functools.partial(per_device, holders=mesh.shape["graph"], depth=mesh.shape["dp"]),
        mesh=mesh,
        in_specs=placed,
        out_specs=(P("dp", "graph", None, None), P("graph", None)),
        check_vma=False,
    )
```

```python
import functools

import jax
import jax.numpy as jnp
from jax import lax
from jax.experimental import pallas as pl
from jax.experimental.pallas import tpu as pltpu
from jax.sharding import PartitionSpec as P

CUTOFF = 12.0
CAP = 24
DEG = 7
COEF = 49
ROWS = 7
CH = 256
WIDTH = DEG * CH
META = 128
HALF = WIDTH // 2
TALL = 112
PARTS = ((0, 384), (384, 512))
SPAN = 64 * ROWS
F32, BF16, I32 = jnp.float32, jnp.bfloat16, jnp.int32
MESH = pl.DeviceIdType.MESH
VMEM_LIMIT = 60 * 1024 * 1024
FAR = (
    (2, 2), (2, 1), (1, 2), (2, 3), (3, 2), (2, 0), (0, 2), (1, 1),
    (3, 3), (1, 3), (3, 1), (1, 0), (0, 1), (3, 0), (0, 3),
)
GROUPS = ((0, 16), (16, 26), (26, 32))
STEPS = [(a, b, c) for c in (0, 1) for a, b in FAR] + [(0, 0, 1)]


def iota(shape, dim):
    return lax.broadcasted_iota(I32, shape, dim)


def onehot(mask):
    return jnp.where(mask, 1.0, 0.0).astype(BF16)


def dot(a, b, dims=((1,), (0,))):
    return lax.dot_general(a, b, (dims, ((), ())), preferred_element_type=F32)


def spread_matrix():
    j, lane = iota((META, SPAN), 0), iota((META, SPAN), 1)
    return onehot((lane & 63 == j) & (j < COEF))


def selector(meta, column):
    wide = dot(meta.astype(BF16), spread_matrix())
    atom = meta[:, column : column + 1].astype(I32)
    return jnp.where(iota(wide.shape, 1) >> 6 == atom, wide, 0.0).astype(BF16)


def in_degree(position, degree):
    return (position >= degree * degree) & (position < (degree + 1) * (degree + 1))


def pack_nodes(nodes_ref, packed_ref):
    packed_ref[...] = jnp.zeros(packed_ref.shape, F32)
    for q in range(ROWS):
        packed_ref[q * 64 : q * 64 + COEF, :] = nodes_ref[q].astype(F32)


def find_meta(holders, count_ref, table_ref, src_ref, tgt_ref, rot_ref, len_ref, turns_ref, turn_ref, rows_ref):
    own = lax.axis_index("graph")
    slots = src_ref.shape[1]
    atoms = table_ref.shape[1]
    live = iota((1, slots), 1) < count_ref[0, 0]
    table = jnp.broadcast_to(table_ref[...].astype(F32), (8, atoms)).astype(BF16)

    def rows_of(ids):
        return dot(table, onehot(iota((atoms, slots), 0) == ids))[0:1].astype(I32)

    src = rows_of(src_ref[...])
    tgt = rows_of(tgt_ref[...])
    holder = (src * 9363) >> 16
    held = onehot((iota((holders, slots), 0) == holder) & live)
    before = onehot(iota((slots, slots), 0) < iota((slots, slots), 1))
    rank = jnp.sum(held.astype(F32) * dot(held, before), axis=0, keepdims=True)
    place = jnp.where(live, holder * CAP + rank.astype(I32), -1)
    chosen = onehot(iota((holders * CAP, slots), 0) == place)

    total = turns_ref[0]
    for degree in range(1, DEG):
        total += turns_ref[degree]
    turn_ref[...] = total
    step = 512
    turned = jnp.zeros((COEF, slots), F32)
    for start in range(0, turns_ref.shape[2], step):
        turned += dot(
            turn_ref[:, start : start + step],
            onehot(iota((step, slots), 0) + start == rot_ref[...]),
        )
    length = len_ref[...]
    high = length.astype(BF16).astype(F32)
    middle = (length - high).astype(BF16).astype(F32)
    rows_ref[...] = jnp.zeros(rows_ref.shape, F32)
    rows_ref[0:COEF, :] = turned
    rows_ref[49:50, :] = (src - holder * ROWS).astype(F32)
    rows_ref[50:51, :] = (tgt - own * ROWS).astype(F32)
    rows_ref[51:52, :] = jnp.ones((1, slots), F32)
    rows_ref[52:53, :] = high
    rows_ref[53:54, :] = middle
    rows_ref[54:55, :] = length - high - middle
    return dot(chosen, rows_ref[...].astype(BF16), ((1,), (1,)))


class PartSum:
    def __init__(self, at, width, own, remote, along, above, layer, depth, partner, site, first, second, core, refs):
        self.at, self.width, self.own, self.remote, self.along, self.above = at, width, own, remote, along, above
        self.site = site
        self.layer, self.depth, self.partner, self.first, self.second, self.core = (
            layer, depth, partner, first, second, core
        )
        (
            self.send1, self.recv1, self.send2, self.recv2, self.total, self.send3, self.recv3,
            self.mine, self.recv4, self.held,
            self.s1, self.r1, self.s2, self.r2, self.s3, self.r3, self.s4, self.r4,
        ) = refs

    def block(self, k, m):
        a, b = lax.rem(self.first + k, 4), lax.rem(self.second + m, 4)
        place = (1 - self.core) * (a * 4 + b) + self.core * (b * 4 + a)
        return self.own[pl.ds(pl.multiple_of(place * TALL, 16), TALL), self.at : self.at + self.width]

    def out1(self, i, k):
        to = k if k != 2 else 1 if i < 2 else 3
        return self.remote(
            self.send1.at[k - 1, i], self.recv1.at[k - 1, i], self.s1.at[k - 1, i], self.r1.at[k - 1, i],
            self.along(to, 0),
        )

    def out2(self, m):
        return self.remote(
            self.send2.at[m - 1], self.recv2.at[m - 1], self.s2.at[m - 1], self.r2.at[m - 1], self.along(0, m)
        )

    def out3(self, k):
        to = lax.rem(self.layer + k, self.depth)
        return self.remote(
            self.send3.at[to], self.recv3.at[k - 1], self.s3.at[k - 1], self.r3.at[k - 1], self.above(k)
        )

    def out4(self, k):
        half = self.depth // 2
        slot = lax.rem(self.layer, half)
        return self.remote(
            self.mine, self.recv4.at[self.core, slot], self.s4.at[k], self.r4.at[self.core, slot],
            {"graph": self.site + self.layer // half, "dp": lax.rem(self.layer + k, self.depth)},
        )

    def is_holder(self):
        return self.layer // (self.depth // 2) == self.core

    def turns(self):
        return sorted(range(1, self.depth), key=lambda k: (-min(k, self.depth - k), k))

    def begin(self):
        for k, i in ((2, 0), (2, 2), (2, 1), (2, 3), (1, 2), (3, 0), (1, 3), (3, 1)):
            self.send1[k - 1, i] = self.block(k, i + 1).astype(BF16)
            self.out1(i, k).start()

    def merge(self):
        for k, i in ((1, 0), (3, 2), (1, 1), (3, 3)):
            self.out1(i, 2).wait_recv()
            self.send1[k - 1, i] = (self.block(k, i + 1) + self.recv1[1, i].astype(F32)).astype(BF16)
            self.out1(i, k).start()

    def gathered(self, i):
        got = self.block(0, i + 1)
        for k in (1, 3):
            self.out1(i, k).wait_recv()
            got += self.recv1[k - 1, i].astype(F32)
        return got

    def second_axis(self):
        for m in (1, 3, 2):
            self.send2[m - 1] = self.gathered(m - 1).astype(BF16)
            self.out2(m).start()
        self.held[...] = self.gathered(3)

    def over_layers(self):
        kept = self.held[...]
        for m in (1, 2, 3):
            self.out2(m).wait_recv()
            kept += self.recv2[m - 1].astype(F32)
        half, mid = TALL // 2, self.total.shape[0] // 2
        self.total[...] = jnp.zeros(self.total.shape, F32)
        self.total[0:half, :] = kept[0:half]
        self.total[mid : mid + half, :] = kept[half:]
        self.send3[...] = self.total[...].astype(BF16).reshape(self.send3.shape)
        for k in self.turns():
            self.out3(k).start()

    def share(self):
        part = self.total[pl.ds(pl.multiple_of(self.layer * 16, 16), 16), :]
        for k in range(1, self.depth):
            self.out3(k).wait_recv()
            part += self.recv3[k - 1].astype(F32)
        self.mine[...] = part.astype(BF16)
        for k in self.turns():
            self.out4(k).start()

        @pl.when(jnp.logical_not(self.is_holder()))
        def _():
            self.out4(0).start()

        @pl.when(self.is_holder())
        def _():
            self.recv4[self.core, lax.rem(self.layer, self.depth // 2)] = self.mine[...]

    def finish(self, out_ref):
        half = self.depth // 2
        for kind in (0, 1):
            for slot in range(half):
                here = (self.core * half + slot == self.layer) & (self.core == kind)

                @pl.when(jnp.logical_not(here))
                def _(kind=kind, slot=slot):
                    self.remote(
                        self.mine, self.recv4.at[kind, slot], self.s4.at[0], self.r4.at[kind, slot], self.partner
                    ).wait_recv()

                tall = min(16, out_ref.shape[0] - slot * 16)
                at = kind * HALF + self.at
                rows = self.recv4[kind, slot].astype(F32)
                out_ref[slot * 16 : slot * 16 + tall, at : at + self.width] = rows[0:tall]

    def sent_chips(self):
        for k in (1, 2, 3):
            for i in range(4):
                self.out1(i, k).wait_send()
            self.out2(k).wait_send()

    def sent_layers(self):
        for k in range(1, self.depth):
            self.out3(k).wait_send()

    def sent_holders(self):
        for k in range(1, self.depth):
            self.out4(k).wait_send()

        @pl.when(jnp.logical_not(self.is_holder()))
        def _():
            self.out4(0).wait_send()


def part_scratch(width, depth):
    block, thin = (TALL, width), (16, width)
    dma = pltpu.SemaphoreType.DMA
    return [
        pltpu.VMEM((3, 4, *block), BF16),
        pltpu.VMEM((3, 4, *block), BF16),
        pltpu.VMEM((3, *block), BF16),
        pltpu.VMEM((3, *block), BF16),
        pltpu.VMEM((depth * 16, width), F32),
        pltpu.VMEM((depth, *thin), BF16),
        pltpu.VMEM((depth - 1, *thin), BF16),
        pltpu.VMEM(thin, BF16),
        pltpu.VMEM((2, depth // 2, *thin), BF16),
        pltpu.VMEM(block, F32),
        dma((3, 4)), dma((3, 4)),
        dma((3,)), dma((3,)),
        dma((depth - 1,)), dma((depth - 1,)),
        dma((depth,)), dma((2, depth // 2)),
    ]


def layer_kernel(
    holders, depth,
    count_ref, table_ref, src_ref, tgt_ref, rot_ref, len_ref, turns_ref, grads_ref, feats_ref, radial_ref, w_hbm,
    node_ref, out_ref,
    turn_ref, rows_ref, packed_ref, meta_out, meta_in, grad_out, grad_in, w_ref,
    grad_ref, in_ref, pick_ref, scale_ref, acc_ref, own_ref, in_peer, grad_peer, half_in,
    ws, ms, mr, gs, gr, is_, ir, hs, hr, *sums,
):
    me, layer = lax.axis_index("graph"), lax.axis_index("dp")
    core, place = lax.rem(me, 2), me // 2
    x, y = place // 4, lax.rem(place, 4)
    rows = holders * CAP
    first = (1 - core) * x + core * y
    second = (1 - core) * y + core * x

    def chip(kind, a, b):
        return (1 - kind) * (a * 4 + b) + kind * (b * 4 + a)

    def index(a, b, c):
        return chip(core, lax.rem(first + a, 4), lax.rem(second + b, 4)) * 2 + lax.rem(core + c, 2)

    def along(a, b):
        return {"graph": index(a, b, 0)}

    partner = {"graph": index(0, 0, 1)}

    def above(k):
        return {"dp": lax.rem(layer + k, depth)}

    def remote(src, dst, ss, rs, peer):
        return pltpu.make_async_remote_copy(
            src_ref=src, dst_ref=dst, send_sem=ss, recv_sem=rs, device_id=peer, device_id_type=MESH
        )

    load_w = pltpu.make_async_copy(w_hbm, w_ref, ws)
    load_w.start()
    barrier = pltpu.get_barrier_semaphore()
    for a, b, c in STEPS:
        pl.semaphore_signal(barrier, inc=1, device_id={"graph": index(a, b, c)}, device_id_type=MESH)
    for k in range(1, depth):
        pl.semaphore_signal(barrier, inc=1, device_id=above(k), device_id_type=MESH)
        pl.semaphore_signal(barrier, inc=1, device_id={**partner, **above(k)}, device_id_type=MESH)

    meta = find_meta(
        holders, count_ref, table_ref, src_ref, tgt_ref, rot_ref, len_ref, turns_ref, turn_ref, rows_ref
    )
    meta_out[...] = meta.reshape(holders, CAP, META).astype(BF16)
    pl.semaphore_wait(barrier, len(STEPS) + 2 * (depth - 1))

    def meta_copy(k):
        peer = index(*STEPS[k - 1])
        return remote(meta_out.at[peer], meta_in.at[k], ms.at[k], mr.at[k], {"graph": peer})

    def grad_copy(k):
        peer = index(*STEPS[k - 1])
        return remote(grad_out.at[peer], grad_in.at[k], gs.at[k], gr.at[k], {"graph": peer})

    for k in range(1, holders):
        meta_copy(k).start()
    pack_nodes(grads_ref, packed_ref)
    pick = selector(meta, 50)
    position = iota((SPAN, CH), 0) & 63
    for degree in range(DEG):
        part = jnp.where(in_degree(position, degree), packed_ref[...], 0.0).astype(BF16)
        grad = dot(pick, part)
        grad_out[:, :, degree * CH : (degree + 1) * CH] = grad.reshape(holders, CAP, CH).astype(BF16)
    for k in range(1, holders):
        grad_copy(k).start()
    meta_in[0] = meta_out[me]
    grad_in[0] = grad_out[me]

    for k in range(1, holders):
        meta_copy(k).wait_recv()
    meta = meta_in[...].astype(F32).reshape(rows, META)
    lane = iota((rows, META), 1)
    length = jnp.sum(jnp.where((lane >= 52) & (lane < 55), meta, 0.0), axis=1, keepdims=True)
    live = meta[:, 51:52]
    gauss = radial_ref.shape[0]
    spacing = CUTOFF / (gauss - 1)
    centers = iota((1, gauss), 1).astype(F32) * spacing
    basis = jnp.exp((-0.5 / (2.0 * spacing) ** 2) * (length - centers) ** 2)
    scale_ref[...] = live * lax.dot_general(
        basis, radial_ref[...], (((1,), (0,)), ((), ())),
        precision=lax.Precision.HIGHEST, preferred_element_type=F32,
    )
    pick = selector(meta, 49)
    pick_ref[...] = pick.astype(F32).T.astype(BF16)
    pack_nodes(feats_ref, packed_ref)
    for degree in range(DEG):
        part = jnp.where(in_degree(position, degree), packed_ref[...], 0.0).astype(BF16)
        edge_in = dot(pick, part) * scale_ref[...]
        in_ref[degree * CH : (degree + 1) * CH, :] = edge_in.T.astype(BF16)
    acc_ref[...] = jnp.zeros(acc_ref.shape, F32)

    def columns(kind):
        return pl.ds(pl.multiple_of(kind * HALF, 128), HALF)

    in_copy = remote(in_ref, in_peer, is_, ir, partner)
    in_copy.start()

    def half_copy(n):
        slabs = pl.ds(GROUPS[n][0], GROUPS[n][1] - GROUPS[n][0])
        return remote(
            grad_in.at[slabs, :, columns(1 - core)], half_in.at[slabs], hs.at[n], hr.at[n], partner
        )

    def arrive(n):
        begin, end = GROUPS[n]
        for k in range(max(begin, 1), end):
            grad_copy(k).wait_recv()
        half_copy(n).start()
        for degree in range(DEG):
            cols = slice(degree * CH, (degree + 1) * CH)
            slab = grad_in[begin:end, :, cols].astype(F32)
            grad_ref[begin * CAP : end * CAP, cols] = slab.reshape(-1, CH).astype(BF16)

    def arrive_peer(n):
        begin, end = GROUPS[n]
        half_copy(n).wait_recv()
        for at, width in PARTS:
            slab = half_in[begin:end, :, at : at + width].astype(F32)
            grad_peer[begin * CAP : end * CAP, at : at + width] = slab.reshape(-1, width).astype(BF16)

    def weights(p, own, peer):
        cols = pl.ds(pl.multiple_of(core * HALF + p.at, 128), p.width)
        there = slice(p.at, p.at + p.width)

        def terms(t, _):
            tall = pl.ds(pl.multiple_of(t * (WIDTH // 2), 128), WIDTH // 2)
            if own:
                term = dot(in_ref[tall, :], grad_ref[:, cols])
            else:
                term = own_ref[tall, there]
            if peer:
                term += dot(in_peer[tall, :], grad_peer[:, there])
            own_ref[tall, there] = term
            return 0

        lax.fori_loop(0, 2, terms, 0)

    def backward(degree, _):
        at = pl.ds(pl.multiple_of(degree * CH, CH), CH)
        hidden = dot(grad_ref[...], w_ref[at, :], ((1,), (1,)))
        back = (hidden * scale_ref[...]).astype(BF16)
        term = dot(pick_ref[...], back)
        acc_ref[...] += jnp.where(in_degree(position, degree), term, 0.0)
        return 0

    each = len(sums) // len(PARTS)
    parts = [
        PartSum(at, width, own_ref, remote, along, above, layer, depth, partner, place * 2, first, second, core,
                sums[n * each : (n + 1) * each])
        for n, (at, width) in enumerate(PARTS)
    ]
    arrive(0)
    arrive(1)
    arrive_peer(0)
    arrive(2)
    weights(parts[0], True, False)
    in_copy.wait_recv()
    arrive_peer(1)
    arrive_peer(2)
    weights(parts[0], False, True)
    parts[0].begin()
    weights(parts[1], True, True)
    parts[1].begin()
    parts[0].merge()
    load_w.wait()
    lax.fori_loop(0, 3, backward, 0)
    parts[1].merge()
    lax.fori_loop(3, 5, backward, 0)
    parts[0].second_axis()
    lax.fori_loop(5, DEG, backward, 0)
    for q in range(ROWS):
        node_ref[q] = acc_ref[q * 64 : q * 64 + COEF, :]
    parts[0].over_layers()
    for k in range(1, holders):
        meta_copy(k).wait_send()
        grad_copy(k).wait_send()
    in_copy.wait_send()
    for n in range(len(GROUPS)):
        half_copy(n).wait_send()
    parts[1].second_axis()
    parts[0].share()
    parts[0].sent_chips()
    parts[1].over_layers()
    parts[0].sent_layers()
    parts[1].sent_chips()
    parts[0].finish(out_ref)
    parts[1].share()
    parts[0].sent_holders()
    parts[1].sent_layers()
    parts[1].finish(out_ref)
    parts[1].sent_holders()


def per_device(
    node_feats, node_grads, node_row, edge_src, edge_tgt, edge_rot, edge_len, edge_count, rotations, w_zero, w_radial,
    holders, depth,
):
    slots = edge_src.shape[1]
    turns = rotations.transpose(1, 2, 0)
    rows = holders * CAP
    vmem = pl.BlockSpec(memory_space=pltpu.VMEM)
    dma = pltpu.SemaphoreType.DMA
    buffer = pltpu.VMEM
    node, weight = pl.pallas_call(
        functools.partial(layer_kernel, holders, depth),
        out_shape=(
            jax.ShapeDtypeStruct((ROWS, COEF, CH), F32),
            jax.ShapeDtypeStruct((WIDTH // holders, WIDTH), F32),
        ),
        in_specs=[pl.BlockSpec(memory_space=pltpu.SMEM)] + [vmem] * 9 + [pl.BlockSpec(memory_space=pl.ANY)],
        out_specs=(vmem, vmem),
        scratch_shapes=[
            buffer((COEF, turns.shape[2]), BF16),
            buffer((META, slots), F32),
            buffer((SPAN, CH), F32),
            buffer((holders, CAP, META), BF16),
            buffer((holders, CAP, META), BF16),
            buffer((holders, CAP, WIDTH), BF16),
            buffer((holders, CAP, WIDTH), BF16),
            buffer((WIDTH, WIDTH), BF16),
            buffer((rows, WIDTH), BF16),
            buffer((WIDTH, rows), BF16),
            buffer((SPAN, rows), BF16),
            buffer((rows, CH), F32),
            buffer((SPAN, CH), F32),
            buffer((WIDTH, HALF), F32),
            buffer((WIDTH, rows), BF16),
            buffer((rows, HALF), BF16),
            buffer((holders, CAP, HALF), BF16),
            dma,
            dma((holders,)), dma((holders,)),
            dma((holders,)), dma((holders,)),
            dma, dma,
            dma((len(GROUPS),)), dma((len(GROUPS),)),
            *(shape for _, width in PARTS for shape in part_scratch(width, depth)),
        ],
        compiler_params=pltpu.CompilerParams(
            collective_id=0, has_side_effects=True, vmem_limit_bytes=VMEM_LIMIT
        ),
        name="layer",
    )(
        edge_count, node_row, edge_src, edge_tgt, edge_rot, edge_len, turns,
        node_grads[0], node_feats[0], w_radial, w_zero,
    )
    return (node[None], weight)


def solution(mesh):
    graph = P("dp", "graph")
    placed = (
        P("dp", "graph", None, None), P("dp", "graph", None, None), P("dp", None),
        graph, graph, graph, graph, graph, P(), P(), P(),
    )
    return jax.shard_map(
        functools.partial(per_device, holders=mesh.shape["graph"], depth=mesh.shape["dp"]),
        mesh=mesh,
        in_specs=placed,
        out_specs=(P("dp", "graph", None, None), P("graph", None)),
        check_vma=False,
    )
```
